512 devices in a mesh: grp: 16 (over z_hi, y), blk: 32 (over x, z_lo, core).
Axes of the slice: x: 4, y: 8, z: 8 (z_hi: 2, z_lo: 4; z = z_hi * 4 + z_lo), core: 2. Of those that a mesh axis runs over, the one named last changes fastest.
Arguments:
- recorded: float32 [65536, 4096], P('grp', 'blk'), may hold values from -320 to 320
- slot_time: int32 [32], replicated, may hold values from 0 to 31, as said below
- passed: int32 [4, 65536], P(None, ('grp', 'blk')), may hold values from 0 to 1, as said below
- round_order: int32 [8], replicated, may hold values from 0 to 7, each once
Outputs:
- correlations: float32 [8, 65536, 512], P(None, ('grp', 'blk'))
The draws below stay inside these ranges and needn't reach their ends.
Inputs may be any that keep to these rules, and one draw needn't show every extreme that they name: `slot_time`: a permutation of 0 to 31. 1 marks a segment of a channel that passed quality control. `round_order`: a permutation of 0 to 7.
All inputs are finite; a program needn't handle non-finite values.
Results may differ from the reference program's by a relative error of at most 0.0036.
Values may be sent and summed in bfloat16 or wider, within the bound.
No kernel may reach another device: no remote copies, remote signals or barrier semaphores. Data moves between devices by JAX's collectives and lax.ppermute only.
A program may use at most 64 MiB of HBM per device.

```python
import math
import jax
import jax.numpy as jnp
from jax import lax

BLOCK = 128
SEGS = 4
SAMPLES = 1024
LAGS = 512
HALF = 64
REACH = 8
FREQS = 512
TIMES = 4096
SLOTS = 32
CHANNELS = 65536


def common_slots(key):
    return jax.random.permutation(jax.random.fold_in(key, 11), SLOTS).astype(jnp.int32)


def draw_slot_time(key, part):
    return common_slots(key)


def draw_recorded(key, part):
    slot_order = common_slots(key)
    slice_len = TIMES // SLOTS
    column = jnp.arange(TIMES, dtype=jnp.int32)
    real_time = slot_order[column // slice_len] * slice_len + column % slice_len
    within = real_time % SAMPLES
    keys = jax.random.split(jax.random.fold_in(key, 23), 5)
    signal = jnp.clip(jax.random.normal(keys[0], (CHANNELS, TIMES), jnp.float32), -5.0, 5.0)
    gain_low = 0.3
    gain_high = 3.0
    scale_high = 10.0
    line_bins = jax.random.randint(keys[1], (CHANNELS, 3), 4, FREQS - 4)
    line_gain = jnp.exp(jax.random.uniform(keys[2], (CHANNELS, 3), jnp.float32, math.log(gain_low), math.log(gain_high)))
    line_phase = jax.random.uniform(keys[3], (CHANNELS, 3), jnp.float32, -math.pi, math.pi)
    for line in range(3):
        angle = jnp.mod(line_bins[:, line:line + 1] * within[None, :], SAMPLES).astype(jnp.float32) * (2.0 * math.pi / SAMPLES)
        signal = signal + line_gain[:, line:line + 1] * jnp.cos(angle + line_phase[:, line:line + 1])
    channel_scale = jnp.exp(jax.random.uniform(keys[4], (CHANNELS, 1), jnp.float32, 0.0, math.log(scale_high)))
    return signal * channel_scale


def draw_passed(key, part):
    keys = jax.random.split(jax.random.fold_in(key, 31), 2)
    pass_level = jax.random.randint(keys[0], (1, CHANNELS // BLOCK), 1, 5)
    level_cols = jnp.repeat(pass_level, BLOCK, axis=1)
    dice_roll = jax.random.randint(keys[1], (SEGS, CHANNELS), 0, 4)
    return (dice_roll < level_cols).astype(jnp.int32)


def setup_inputs(seed: int = 0) -> dict:
    arg_keys = jax.random.split(jax.random.key(seed), 5)
    return {
        "recorded": draw_recorded(jax.random.fold_in(arg_keys[4], 71), 0),
        "slot_time": draw_slot_time(jax.random.fold_in(arg_keys[4], 71), 0),
        "passed": draw_passed(jax.random.fold_in(arg_keys[4], 71), 0),
        "round_order": jax.random.permutation(arg_keys[3], REACH).astype(jnp.int32),
    }


EPSILON = 1e-05

def lag_table():
    freq_index = jnp.arange(FREQS, dtype=jnp.int32)
    lag_index = jnp.arange(LAGS, dtype=jnp.int32) - LAGS // 2
    phase_angle = jnp.mod(freq_index[:, None] * lag_index[None, :], SAMPLES).astype(jnp.float32) * (2.0 * math.pi / SAMPLES)
    weight = jnp.where(freq_index == 0, 1.0, 2.0).astype(jnp.float32)[:, None]
    return jnp.concatenate([weight * jnp.cos(phase_angle), -weight * jnp.sin(phase_angle)], axis=0)

def band_table():
    freq_index = jnp.arange(FREQS, dtype=jnp.int32)
    band_mask = (jnp.abs(freq_index[:, None] - freq_index[None, :]) <= HALF).astype(jnp.float32)
    return (band_mask, lax.optimization_barrier(jnp.sum(band_mask, axis=0)))

def whiten_group(series):
    members = series.shape[0]
    segment = series.reshape(members, SEGS, SAMPLES)
    segment = segment - lax.optimization_barrier(jnp.mean(segment, axis=2, keepdims=True))
    spectrum = jnp.fft.rfft(segment, axis=2)[:, :, :FREQS]
    real_part = jnp.real(spectrum).astype(jnp.float32)
    imag_part = jnp.imag(spectrum).astype(jnp.float32)
    magnitude = jnp.sqrt(real_part * real_part + imag_part * imag_part)
    band_mask, band_size = band_table()
    smooth = jnp.dot(magnitude.reshape(-1, FREQS), band_mask, precision=lax.Precision.HIGHEST) / band_size
    scale = 1.0 / (smooth.reshape(members, SEGS, FREQS) + EPSILON)
    return jnp.concatenate([real_part * scale, imag_part * scale], axis=2).astype(jnp.bfloat16)

def reference(recorded, slot_time, passed, round_order):
    channel_count = recorded.shape[0]
    slices = recorded.reshape(channel_count, SLOTS, TIMES // SLOTS)
    ordered = jnp.zeros_like(slices).at[:, slot_time, :].set(slices).reshape(channel_count, TIMES)
    groups = ordered.reshape(channel_count // (BLOCK * SLOTS), BLOCK * SLOTS, TIMES)
    whitened = lax.map(whiten_group, groups).reshape(channel_count, SEGS, 2 * FREQS)
    passes = jnp.transpose(passed).astype(jnp.float32)
    white_pad = jnp.concatenate([whitened, jnp.zeros((REACH * BLOCK, SEGS, 2 * FREQS), jnp.bfloat16)], axis=0)
    passes_pad = jnp.concatenate([passes, jnp.zeros((REACH * BLOCK, SEGS), jnp.float32)], axis=0)
    own_re = whitened[:, :, :FREQS].astype(jnp.float32)
    own_im = whitened[:, :, FREQS:].astype(jnp.float32)
    table = lag_table()
    results = []
    for offset in range(1, REACH + 1):
        partner = white_pad[offset * BLOCK:offset * BLOCK + channel_count]
        partner_re = partner[:, :, :FREQS].astype(jnp.float32)
        partner_im = partner[:, :, FREQS:].astype(jnp.float32)
        weight = passes * passes_pad[offset * BLOCK:offset * BLOCK + channel_count]
        cross_re = lax.optimization_barrier(jnp.sum(weight[:, :, None] * (own_re * partner_re + own_im * partner_im), axis=1))
        cross_im = lax.optimization_barrier(jnp.sum(weight[:, :, None] * (own_re * partner_im - own_im * partner_re), axis=1))
        members = lax.optimization_barrier(jnp.sum(weight, axis=1))
        lagged = jnp.dot(jnp.concatenate([cross_re, cross_im], axis=1), table, precision=lax.Precision.HIGHEST)
        results.append(lagged / (math.sqrt(SAMPLES) * jnp.maximum(members, 1.0))[:, None])
    stacked = jnp.stack(results)
    return jnp.take(stacked, round_order, axis=0)
```

```python
import math

import jax
import jax.numpy as jnp
import numpy as np
from jax import lax
from jax.sharding import PartitionSpec as P

BLOCK = 128
SEGS = 4
SAMPLES = 1024
LAGS = 512
HALF = 64
REACH = 8
FREQS = 512


EPSILON = 1e-05


def fourier_table():
    time_index = np.arange(SAMPLES)
    freq_index = np.arange(FREQS)
    angle = (time_index[:, None] * freq_index[None, :] % SAMPLES) * (2.0 * math.pi / SAMPLES)
    return np.concatenate([np.cos(angle), -np.sin(angle)], axis=1).astype(np.float32)


def lag_table():
    freq_index = np.arange(FREQS)
    lag_index = np.arange(LAGS) - LAGS // 2
    angle = (freq_index[:, None] * lag_index[None, :] % SAMPLES) * (2.0 * math.pi / SAMPLES)
    weight = np.where(freq_index == 0, 1.0, 2.0)[:, None] / math.sqrt(SAMPLES)
    return np.concatenate([weight * np.cos(angle), -weight * np.sin(angle)], axis=0).astype(np.float32)


def band_table():
    freq_index = np.arange(FREQS)
    mask = np.abs(freq_index[:, None] - freq_index[None, :]) <= HALF
    return mask.astype(np.float32), mask.sum(axis=0).astype(np.float32)


def per_device(recorded, slot_time, passed, round_order):
    teams = lax.axis_size("blk")
    groups = lax.axis_size("grp")
    places = BLOCK // teams
    rows = teams * places
    me = lax.axis_index("blk")
    route = [(g, g - 1) for g in range(1, groups)]

    slot_index = jnp.arange(teams, dtype=jnp.int32)
    inverse = jnp.sum(
        jnp.where(slot_time[None, :] == slot_index[:, None], slot_index[None, :], 0), axis=1
    )
    pieces = jnp.transpose(recorded.reshape(teams, teams, places, -1), (1, 0, 2, 3))
    pieces = pieces.reshape(teams, rows, -1)
    received = lax.all_to_all(pieces, "blk", split_axis=0, concat_axis=0, tiled=True)

    flags = lax.all_gather(passed.astype(jnp.float32), "blk")
    flags = lax.dynamic_slice_in_dim(flags, me * places, places, axis=2)
    flags = jnp.transpose(flags, (1, 0, 2))
    flags_halo = lax.ppermute(flags[:, :REACH], "grp", route)
    flags_all = jnp.concatenate([flags, flags_halo], axis=1)

    series = jnp.take(received, inverse, axis=0).reshape(SEGS, -1, rows, received.shape[2])
    segment = jnp.transpose(series, (0, 2, 1, 3)).reshape(SEGS, rows, SAMPLES)
    segment = segment - jnp.mean(segment, axis=2, keepdims=True)
    flat_rows = segment.reshape(SEGS * rows, SAMPLES)
    spectrum = jnp.dot(flat_rows, fourier_table(), precision=lax.Precision.HIGHEST)
    real_part = spectrum[:, :FREQS]
    imag_part = spectrum[:, FREQS:]
    magnitude = jnp.sqrt(real_part * real_part + imag_part * imag_part)
    band_mask, band_size = band_table()
    smooth = jnp.dot(magnitude, band_mask, precision=lax.Precision.HIGHEST) / band_size
    scale = 1.0 / (smooth + EPSILON)
    whitened = spectrum * jnp.concatenate([scale, scale], axis=1)
    whitened = whitened.reshape(SEGS, teams, places, 2 * FREQS) * flags[:, :, :, None]
    whitened = whitened.astype(jnp.bfloat16)
    halo = lax.ppermute(whitened[:, :REACH], "grp", route)
    whole = jnp.concatenate([whitened, halo], axis=1).astype(jnp.float32)
    own = whole[:, :teams]
    spectra = []
    totals = []
    for offset in range(1, REACH + 1):
        partner = whole[:, offset:offset + teams]
        cross_re = jnp.sum(
            own[..., :FREQS] * partner[..., :FREQS] + own[..., FREQS:] * partner[..., FREQS:], axis=0
        )
        cross_im = jnp.sum(
            own[..., :FREQS] * partner[..., FREQS:] - own[..., FREQS:] * partner[..., :FREQS], axis=0
        )
        spectra.append(jnp.concatenate([cross_re, cross_im], axis=-1))
        totals.append(jnp.sum(flags * flags_all[:, offset:offset + teams], axis=0))
    spectra = jnp.stack(spectra).reshape(REACH * rows, 2 * FREQS)
    lagged = jnp.dot(spectra, lag_table(), precision=lax.Precision.HIGHEST)
    lagged = lagged.reshape(REACH, teams, places, LAGS)
    lagged = lagged / jnp.maximum(jnp.stack(totals), 1.0)[..., None]
    sent = jnp.transpose(lagged.astype(jnp.bfloat16), (1, 0, 2, 3)).reshape(teams, REACH * places, LAGS)
    owned = lax.all_to_all(sent, "blk", split_axis=0, concat_axis=0, tiled=True)
    owned = owned.reshape(teams, REACH, places, LAGS)
    owned = jnp.take(owned, round_order, axis=1)
    return jnp.transpose(owned, (1, 0, 2, 3)).reshape(REACH, BLOCK, LAGS).astype(jnp.float32)


def solution(mesh):
    return jax.shard_map(
        per_device,
        mesh=mesh,
        in_specs=(P("grp", "blk"), P(), P(None, ("grp", "blk")), P()),
        out_specs=P(None, ("grp", "blk"), None),
        check_vma=False,
    )
```

```python
import functools
import math

import jax
import jax.numpy as jnp
import numpy as np
from jax import lax
from jax.experimental import pallas as pl
from jax.experimental.pallas import tpu as pltpu
from jax.sharding import PartitionSpec as P

BLOCK = 128
SEGS = 4
SAMPLES = 1024
SLICE = 128
LAGS = 512
HALF = 64
REACH = 8
FREQS = 512
TEAMS = 32
PLACES = BLOCK // TEAMS
ROWS = TEAMS * PLACES
HALO = REACH * PLACES
WIDTH = 2 * FREQS + 128
LANES = 128
EPSILON = 1e-05
F32 = jnp.float32
BF16 = jnp.bfloat16

BINS = np.concatenate([np.arange(0, FREQS, 2), np.arange(1, FREQS, 2)])


def split3(table):
    terms = []
    rest = table.astype(np.float32)
    for _ in range(3):
        term = rest.astype(BF16)
        terms.append(term)
        rest = rest - term.astype(np.float32)
    return terms


def fourier_tables():
    time_index = np.arange(SAMPLES // 2)
    tables = []
    for first in range(2):
        bins = np.arange(first, FREQS, 2)
        angle = (time_index[:, None] * bins[None, :] % SAMPLES) * (2.0 * math.pi / SAMPLES)
        tables.append(split3(np.concatenate([np.cos(angle), -np.sin(angle)], axis=1)))
    return np.stack([np.stack(terms) for terms in tables])


def lag_tables():
    lag_index = np.arange(LAGS) - LAGS // 2
    angle = (BINS[:, None] * lag_index[None, :] % SAMPLES) * (2.0 * math.pi / SAMPLES)
    weight = np.where(BINS == 0, 1.0, 2.0)[:, None] / math.sqrt(SAMPLES)
    table = np.concatenate([weight * np.cos(angle), -weight * np.sin(angle)], axis=0)
    return np.stack(split3(table)[:2])


def band_tables():
    mask = np.abs(BINS[:, None] - BINS[None, :]) <= HALF
    return mask.astype(BF16), (1.0 / mask.sum(axis=0)).astype(np.float32)[None, :]


def low_half(shape):
    return lax.broadcasted_iota(jnp.int32, shape, len(shape) - 2) % 8 < 4


def swap(x):
    return pltpu.roll(x, 4, len(x.shape) - 2)


def exchange(first, second):
    low = low_half(first.shape)
    return jnp.where(low, first, swap(second)), jnp.where(low, swap(first), second)


def dot(a, b):
    return jnp.dot(a, b, preferred_element_type=F32)


def pack_kernel(recorded_ref, passed_ref, pieces_ref):
    spot = lax.broadcasted_iota(jnp.int32, (BLOCK, LANES), 0)
    lane = lax.broadcasted_iota(jnp.int32, (BLOCK, LANES), 1)
    flags = jnp.zeros((BLOCK, LANES), F32)
    for seg in range(SEGS):
        line = passed_ref[seg:seg + 1, :].astype(F32)
        column = jnp.sum(jnp.where(spot == lane, line, 0.0), axis=1, keepdims=True)
        flags = jnp.where(lane // (LANES // SEGS) == seg, column, flags)
    for tile in range(BLOCK // 8):
        part = flags[8 * tile:8 * tile + 8]
        even, odd = exchange(part, part)
        pieces_ref[2 * tile, ROWS:] = even
        pieces_ref[2 * tile + 1, ROWS:] = odd
        for pair in range(TEAMS // 2):
            start = 2 * pair * BLOCK + 8 * tile
            even, odd = exchange(
                recorded_ref[start:start + 8], recorded_ref[start + BLOCK:start + BLOCK + 8]
            )
            pieces_ref[2 * tile, 8 * pair:8 * pair + 8] = even
            pieces_ref[2 * tile + 1, 8 * pair:8 * pair + 8] = odd


def pack(recorded, passed):
    return pl.pallas_call(
        pack_kernel,
        out_shape=jax.ShapeDtypeStruct((TEAMS, ROWS + 8, SLICE), F32),
        compiler_params=pltpu.CompilerParams(vmem_limit_bytes=16 * 2**20),
        cost_estimate=pl.CostEstimate(flops=2**20, bytes_accessed=2**22, transcendentals=0),
    )(recorded, passed)


def flag_tile(received_ref, pair, seg):
    even = received_ref[2 * pair, ROWS:]
    odd = received_ref[2 * pair + 1, ROWS:]
    both = jnp.where(low_half(even.shape), even, odd)
    column = both[:, seg * (LANES // SEGS):seg * (LANES // SEGS) + 1]
    return jnp.broadcast_to(column, (8, LANES))


def whiten_kernel(
    first, count, slot_ref, received_ref, fourier_ref, band_ref, size_ref, white_ref, place_ref, sum_ref, diff_ref,
    flag_ref
):
    for a in range(TEAMS):
        place_ref[slot_ref[a]] = a
    slices = SAMPLES // SLICE
    half = slices // 2
    for seg in range(SEGS):
        rows = pl.ds(seg * count, count)
        for j in range(half):
            a = received_ref[place_ref[seg * slices + j], first:first + count]
            b = received_ref[place_ref[seg * slices + j + half], first:first + count]
            sum_ref[rows, j * SLICE:(j + 1) * SLICE] = a + b
            diff_ref[rows, j * SLICE:(j + 1) * SLICE] = a - b
        for pair in range(count // 8):
            flag_ref[seg * count + 8 * pair:seg * count + 8 * pair + 8] = flag_tile(
                received_ref, first // 8 + pair, seg
            )
    chunk = 128
    quarter = FREQS // 2

    def body(step):
        rows = pl.ds(pl.multiple_of(step * chunk, chunk), chunk)

        def transform(x, which):
            x1 = x.astype(BF16)
            rest = x - x1.astype(F32)
            x2 = rest.astype(BF16)
            x3 = (rest - x2.astype(F32)).astype(BF16)
            t1, t2, t3 = (fourier_ref[which, i] for i in range(3))
            small = dot(x1, t3) + dot(x3, t1) + dot(x2, t2)
            return dot(x1, t1) + ((dot(x1, t2) + dot(x2, t1)) + small)

        total = sum_ref[rows]
        mean = jnp.sum(total, axis=1, keepdims=True) * (1.0 / SAMPLES)
        even = transform(total - 2.0 * mean, 0)
        odd = transform(diff_ref[rows], 1)
        parts = (even[:, :quarter], odd[:, :quarter], even[:, quarter:], odd[:, quarter:])
        magnitude = jnp.concatenate(
            [
                jnp.sqrt(parts[0] * parts[0] + parts[2] * parts[2]),
                jnp.sqrt(parts[1] * parts[1] + parts[3] * parts[3]),
            ],
            axis=1,
        )
        large = magnitude.astype(BF16)
        small = (magnitude - large.astype(F32)).astype(BF16)
        level = (dot(large, band_ref[...]) + dot(small, band_ref[...])) * size_ref[...]
        flags = flag_ref[rows]
        scale = jnp.concatenate([flags] * (FREQS // LANES), axis=1) / (level + EPSILON)
        for i, part in enumerate(parts):
            side = scale[:, (i % 2) * quarter:(i % 2 + 1) * quarter]
            white_ref[rows, i * quarter:(i + 1) * quarter] = (part * side).astype(BF16)
        white_ref[rows, 2 * FREQS:] = flags.astype(BF16)

    pl.loop(0, SEGS * count // chunk)(body)


def whiten(first, count, slot_time, received):
    vmem = pl.BlockSpec(memory_space=pltpu.VMEM)
    band, size = band_tables()
    flops = 2 * SEGS * count * SAMPLES * SAMPLES * 4
    return pl.pallas_call(
        functools.partial(whiten_kernel, first, count),
        out_shape=jax.ShapeDtypeStruct((SEGS * count, WIDTH), BF16),
        in_specs=[pl.BlockSpec(memory_space=pltpu.SMEM)] + [vmem] * 4,
        out_specs=vmem,
        scratch_shapes=[
            pltpu.SMEM((TEAMS,), jnp.int32),
            pltpu.VMEM((SEGS * count, SAMPLES // 2), F32),
            pltpu.VMEM((SEGS * count, SAMPLES // 2), F32),
            pltpu.VMEM((SEGS * count, LANES), F32),
        ],
        compiler_params=pltpu.CompilerParams(vmem_limit_bytes=24 * 2**20),
        cost_estimate=pl.CostEstimate(flops=flops, bytes_accessed=2**23, transcendentals=2**18),
    )(slot_time, received, fourier_tables(), band, size)


def correlate_kernel(sources, first, count, order_ref, *refs):
    own_refs = refs[:len(sources)]
    table_ref, sent_ref, even_ref, odd_ref, cross_ref, scale_ref = refs[len(sources):]
    base = first * PLACES
    rows = count * PLACES
    need = rows + HALO
    for (start, length), ref in zip(sources, own_refs):
        low = max(base, start)
        high = min(base + need, start + length)
        for seg in range(SEGS):
            if low < high:
                x = ref[seg * length + low - start:seg * length + high - start].astype(F32)
                even_ref[seg, low - base:high - base] = x
                if low == base:
                    odd_ref[seg, 0:high - low - 4] = x[4:]
                else:
                    odd_ref[seg, low - base - 4:high - base - 4] = x
    tiles = rows // 8

    def round_body(r):
        place = order_ref[r] + 1
        shifted = place % 2
        start = (place - shifted) * PLACES

        def tile_body(ref):
            for t in range(tiles):
                own_rows = pl.ds(8 * t, 8)
                rows_out = pl.ds(pl.multiple_of(r * rows + 8 * t, 8), 8)
                partner_rows = pl.ds(pl.multiple_of(start + 8 * t, 8), 8)
                members = jnp.zeros((8, LANES), F32)
                for seg in range(SEGS):
                    members += even_ref[seg, own_rows, 2 * FREQS:] * ref[seg, partner_rows, 2 * FREQS:]
                scale_ref[rows_out] = 1.0 / jnp.maximum(members, 1.0)
                for c in range(FREQS // LANES):
                    re = slice(c * LANES, (c + 1) * LANES)
                    im = slice(FREQS + c * LANES, FREQS + (c + 1) * LANES)
                    cross_re = jnp.zeros((8, LANES), F32)
                    cross_im = jnp.zeros((8, LANES), F32)
                    for seg in range(SEGS):
                        own_re = even_ref[seg, own_rows, re]
                        own_im = even_ref[seg, own_rows, im]
                        partner_re = ref[seg, partner_rows, re]
                        partner_im = ref[seg, partner_rows, im]
                        cross_re += own_re * partner_re + own_im * partner_im
                        cross_im += own_re * partner_im - own_im * partner_re
                    for where, value in ((re, cross_re), (im, cross_im)):
                        cross_ref[rows_out, where] = value

        @pl.when(shifted == 0)
        def _():
            tile_body(even_ref)

        @pl.when(shifted == 1)
        def _():
            tile_body(odd_ref)

    pl.loop(0, REACH)(round_body)

    def group_body(g):
        both = []
        for i in range(4):
            at = pl.ds(pl.multiple_of((4 * g + i) * rows, 8), rows)
            cross = cross_ref[at]
            large = cross.astype(BF16)
            small = (cross - large.astype(F32)).astype(BF16)
            lagged = dot(large, table_ref[0]) + (dot(large, table_ref[1]) + dot(small, table_ref[0]))
            scale = scale_ref[at]
            lagged = lagged * jnp.concatenate([scale] * (LAGS // LANES), axis=1)
            both.append(lagged.reshape(tiles, 8, LAGS))
        for side in range(2):
            halves = [exchange(both[2 * k], both[2 * k + 1])[side] for k in range(2)]
            block = jnp.concatenate(halves, axis=1).astype(BF16)
            sent_ref[first // 2:first // 2 + tiles, side, pl.ds(pl.multiple_of(16 * g, 16), 16)] = block

    for g in range(REACH // 4):
        group_body(g)


def correlate_all(round_order, parts):
    vmem = pl.BlockSpec(memory_space=pltpu.VMEM)
    sources = tuple(where for where, _ in parts)
    arrays = [array for _, array in parts]
    first, count = 0, TEAMS
    rows = count * PLACES
    return pl.pallas_call(
        functools.partial(correlate_kernel, sources, first, count),
        out_shape=jax.ShapeDtypeStruct((TEAMS // 2, 2, REACH * PLACES, LAGS), BF16),
        in_specs=[pl.BlockSpec(memory_space=pltpu.SMEM)] + [vmem] * (len(arrays) + 1),
        out_specs=vmem,
        scratch_shapes=[
            pltpu.VMEM((SEGS, rows + HALO, WIDTH), F32),
            pltpu.VMEM((SEGS, rows + HALO, WIDTH), F32),
            pltpu.VMEM((REACH * rows, 2 * FREQS), F32),
            pltpu.VMEM((REACH * rows, LANES), F32),
        ],
        compiler_params=pltpu.CompilerParams(vmem_limit_bytes=48 * 2**20),
        cost_estimate=pl.CostEstimate(
            flops=2 * REACH * rows * SAMPLES * LAGS * 3, bytes_accessed=2**22, transcendentals=0
        ),
    )(round_order, *arrays, lag_tables())


def unpack_kernel(owned_ref, out_ref):
    x = owned_ref[...].astype(F32)
    x = x.reshape(TEAMS // 2, 2, 16, x.shape[2])
    even, odd = x[:, 0], x[:, 1]
    for half in range(2):
        pair = exchange(even[:, 8 * half:8 * half + 8], odd[:, 8 * half:8 * half + 8])
        for i in range(2):
            out_ref[2 * half + i] = pair[i].reshape(BLOCK, -1)


def unpack(owned):
    width = LAGS // 2
    return pl.pallas_call(
        unpack_kernel,
        grid=(REACH // 4, LAGS // width),
        out_shape=jax.ShapeDtypeStruct((REACH, BLOCK, LAGS), F32),
        in_specs=[pl.BlockSpec((TEAMS, 16, width), lambda r, l: (0, r, l))],
        out_specs=pl.BlockSpec((4, BLOCK, width), lambda r, l: (r, 0, l)),
        compiler_params=pltpu.CompilerParams(vmem_limit_bytes=16 * 2**20),
        cost_estimate=pl.CostEstimate(flops=2**20, bytes_accessed=3 * 2**20, transcendentals=0),
    )(owned)


def per_device(recorded, slot_time, passed, round_order):
    groups = lax.axis_size("grp")
    route = [(g, g - 1) for g in range(1, groups)]
    received = lax.all_to_all(pack(recorded, passed), "blk", split_axis=0, concat_axis=0, tiled=True)
    head = whiten(0, HALO, slot_time, received)
    halo = lax.ppermute(head, "grp", route)
    tail = whiten(HALO, ROWS - HALO, slot_time, received)
    parts = [((0, HALO), head), ((HALO, ROWS - HALO), tail), ((ROWS, HALO), halo)]
    sent = correlate_all(round_order, parts).reshape(TEAMS, REACH * PLACES, LAGS)
    owned = lax.all_to_all(sent, "blk", split_axis=0, concat_axis=0, tiled=True)
    return unpack(owned)


def solution(mesh):
    return jax.shard_map(
        per_device,
        mesh=mesh,
        in_specs=(P("grp", "blk"), P(), P(None, ("grp", "blk")), P()),
        out_specs=P(None, ("grp", "blk"), None),
        check_vma=False,
    )
```

```python
import functools
import math

import jax
import jax.numpy as jnp
import numpy as np
from jax import lax
from jax.experimental import pallas as pl
from jax.experimental.pallas import tpu as pltpu
from jax.sharding import PartitionSpec as P

BLOCK = 128
SEGS = 4
SAMPLES = 1024
SLICE = 128
LAGS = 512
HALF = 64
REACH = 8
FREQS = 512
TEAMS = 32
PLACES = BLOCK // TEAMS
ROWS = TEAMS * PLACES
HALO = REACH * PLACES
WIDTH = 2 * FREQS + 128
LANES = 128
TILES = ROWS // 8
WORDS = ROWS * 3 // 4
SCALE_BITS = 22
SCALE_BASE = 128
MIRROR = 6
EPSILON = 1e-05
F32 = jnp.float32
BF16 = jnp.bfloat16

BINS = np.concatenate([np.arange(0, FREQS, 2), np.arange(1, FREQS, 2)])


def split3(table):
    terms = []
    rest = table.astype(np.float32)
    for _ in range(3):
        term = rest.astype(BF16)
        terms.append(term)
        rest = rest - term.astype(np.float32)
    return terms


def fourier_tables():
    time_index = np.arange(SAMPLES // 2)
    tables = []
    for first in range(2):
        bins = np.arange(first, FREQS, 2)
        angle = (time_index[:, None] * bins[None, :] % SAMPLES) * (2.0 * math.pi / SAMPLES)
        tables.append(split3(np.concatenate([np.cos(angle), -np.sin(angle)], axis=1)))
    return np.stack([np.stack(terms) for terms in tables])


def lag_tables():
    lag_index = np.arange(LAGS) - LAGS // 2
    angle = (BINS[:, None] * lag_index[None, :] % SAMPLES) * (2.0 * math.pi / SAMPLES)
    weight = np.where(BINS == 0, 1.0, 2.0)[:, None] / math.sqrt(SAMPLES)
    table = np.concatenate([weight * np.cos(angle), -weight * np.sin(angle)], axis=0)
    return np.stack(split3(table)[:2])


def band_tables():
    mask = np.abs(BINS[:, None] - BINS[None, :]) <= HALF
    return mask.astype(BF16), (1.0 / mask.sum(axis=0)).astype(np.float32)[None, :]


def low_half(shape):
    return lax.broadcasted_iota(jnp.int32, shape, len(shape) - 2) % 8 < 4


def swap(x):
    return pltpu.roll(x, 4, len(x.shape) - 2)


def exchange(first, second):
    low = low_half(first.shape)
    return jnp.where(low, first, swap(second)), jnp.where(low, swap(first), second)


def dot(a, b):
    return jnp.dot(a, b, preferred_element_type=F32)


def encode(x):
    top = jnp.max(jnp.abs(x), axis=1, keepdims=True)
    exponent = jnp.floor(jnp.log2(jnp.maximum(top, 1e-30))) + 1.0
    limit = 2.0**SCALE_BITS - 1.0
    scaled = jnp.floor(x * jnp.exp2(SCALE_BITS - exponent) + 0.5)
    return jnp.clip(scaled, -limit, limit).astype(jnp.int32), exponent.astype(jnp.int32) + SCALE_BASE


def pack_kernel(flip_ref, recorded_ref, passed_ref, pieces_ref, flags_ref):
    spot = lax.broadcasted_iota(jnp.int32, (BLOCK, LANES), 0)
    lane = lax.broadcasted_iota(jnp.int32, (BLOCK, LANES), 1)
    flags = jnp.zeros((BLOCK, LANES), jnp.int32)
    for seg in range(SEGS):
        line = passed_ref[seg:seg + 1, :].astype(F32)
        column = jnp.sum(jnp.where(spot == lane, line, 0.0), axis=1, keepdims=True)
        flags = jnp.where(lane // TILES == SEGS + seg, column.astype(jnp.int32), flags)
    flags_ref[...] = flags
    lane = lax.broadcasted_iota(jnp.int32, (8, LANES), 1)

    def body(tile):
        part = flags_ref[pl.ds(pl.multiple_of(8 * tile, 8), 8)]
        sides = list(exchange(part, part))
        codes = [[], []]
        for pair in range(TILES):
            start = pl.multiple_of(2 * pair * BLOCK + 8 * tile, 8)
            tiles = exchange(
                recorded_ref[pl.ds(start, 8)],
                recorded_ref[pl.ds(pl.multiple_of(start + BLOCK, 8), 8)],
            )
            for i in range(2):
                code, exponent = encode(tiles[i])
                codes[i].append(code)
                sides[i] = jnp.where(lane == pair, exponent, sides[i])
        for i in range(2):
            target = (2 * tile + i) ^ flip_ref[0]
            for g in range(TILES // 4):
                last = codes[i][4 * g + 3]
                extra = lax.shift_right_logical(sides[i], 4 * g) & 15
                low = (
                    last & 511,
                    lax.shift_right_logical(last, 9) & 511,
                    (lax.shift_right_logical(last, 18) & 31) | (extra << 5),
                )
                for k in range(3):
                    word = (codes[i][4 * g + k] << 9) | low[k]
                    pieces_ref[target, 24 * g + 8 * k:24 * g + 8 * k + 8] = word

    pl.loop(0, BLOCK // 8)(body)


def pack(flip, recorded, passed):
    vmem = pl.BlockSpec(memory_space=pltpu.VMEM)
    return pl.pallas_call(
        pack_kernel,
        out_shape=jax.ShapeDtypeStruct((TEAMS, WORDS, SLICE), jnp.int32),
        in_specs=[pl.BlockSpec(memory_space=pltpu.SMEM), vmem, vmem],
        out_specs=vmem,
        scratch_shapes=[pltpu.VMEM((BLOCK, LANES), jnp.int32)],
        compiler_params=pltpu.CompilerParams(vmem_limit_bytes=16 * 2**20),
        cost_estimate=pl.CostEstimate(flops=2**20, bytes_accessed=2**22, transcendentals=0),
    )(flip, recorded, passed)


def side_tile(received_ref, a):
    low = lax.shift_right_logical(received_ref[a, 16:24], 5) & 15
    high = lax.shift_right_logical(received_ref[a, 40:48], 5) & 15
    return low | (high << 4)


def decode(received_ref, scale_ref, a, g):
    words = [received_ref[a, 24 * g + 8 * k:24 * g + 8 * k + 8] for k in range(3)]
    last = (words[0] & 511) | ((words[1] & 511) << 9) | lax.shift_right_arithmetic(words[2] << 27, 9)
    codes = [lax.shift_right_arithmetic(word, 9) for word in words] + [last]
    scale = scale_ref[a]
    return [
        code.astype(F32) * scale[:, 4 * g + k:4 * g + k + 1] for k, code in enumerate(codes)
    ]


def flag_tile(side_ref, pair, seg):
    even = side_ref[2 * pair]
    odd = side_ref[2 * pair + 1]
    both = jnp.where(low_half(even.shape), even, odd)
    at = (SEGS + seg) * TILES
    return jnp.broadcast_to(both[:, at:at + 1], (8, LANES))


def whiten_kernel(
    first, count, slot_ref, received_ref, fourier_ref, band_ref, size_ref, white_ref, place_ref, sum_ref, diff_ref,
    flag_ref, side_ref, scale_ref
):
    for a in range(TEAMS):
        place_ref[slot_ref[a]] = a
    for a in range(TEAMS):
        side = side_tile(received_ref, a).astype(F32)
        side_ref[a] = side
        scale_ref[a] = jnp.exp2(side - float(SCALE_BASE + SCALE_BITS))
    slices = SAMPLES // SLICE
    half = slices // 2
    for seg in range(SEGS):
        for j in range(half):
            one = place_ref[seg * slices + j]
            other = place_ref[seg * slices + j + half]
            for g in range(count // 32):
                early = decode(received_ref, scale_ref, one, first // 32 + g)
                late = decode(received_ref, scale_ref, other, first // 32 + g)
                for k in range(4):
                    at = seg * count + 32 * g + 8 * k
                    sum_ref[at:at + 8, j * SLICE:(j + 1) * SLICE] = early[k] + late[k]
                    diff_ref[at:at + 8, j * SLICE:(j + 1) * SLICE] = early[k] - late[k]
        for pair in range(count // 8):
            flag_ref[seg * count + 8 * pair:seg * count + 8 * pair + 8] = flag_tile(
                side_ref, first // 8 + pair, seg
            )
    chunk = 128
    quarter = FREQS // 2

    def body(step):
        rows = pl.ds(pl.multiple_of(step * chunk, chunk), chunk)

        def transform(x, which):
            x1 = x.astype(BF16)
            rest = x - x1.astype(F32)
            x2 = rest.astype(BF16)
            x3 = (rest - x2.astype(F32)).astype(BF16)
            t1, t2, t3 = (fourier_ref[which, i] for i in range(3))
            small = dot(x1, t3) + dot(x3, t1) + dot(x2, t2)
            return dot(x1, t1) + ((dot(x1, t2) + dot(x2, t1)) + small)

        total = sum_ref[rows]
        mean = jnp.sum(total, axis=1, keepdims=True) * (1.0 / SAMPLES)
        even = transform(total - 2.0 * mean, 0)
        odd = transform(diff_ref[rows], 1)
        parts = (even[:, :quarter], odd[:, :quarter], even[:, quarter:], odd[:, quarter:])
        magnitude = jnp.concatenate(
            [
                jnp.sqrt(parts[0] * parts[0] + parts[2] * parts[2]),
                jnp.sqrt(parts[1] * parts[1] + parts[3] * parts[3]),
            ],
            axis=1,
        )
        large = magnitude.astype(BF16)
        small = (magnitude - large.astype(F32)).astype(BF16)
        level = (dot(large, band_ref[...]) + dot(small, band_ref[...])) * size_ref[...]
        flags = flag_ref[rows]
        scale = jnp.concatenate([flags] * (FREQS // LANES), axis=1) / (level + EPSILON)
        for i, part in enumerate(parts):
            side = scale[:, (i % 2) * quarter:(i % 2 + 1) * quarter]
            white_ref[rows, i * quarter:(i + 1) * quarter] = (part * side).astype(BF16)
        white_ref[rows, 2 * FREQS:] = flags.astype(BF16)

    pl.loop(0, SEGS * count // chunk)(body)


def whiten(first, count, slot_time, received):
    vmem = pl.BlockSpec(memory_space=pltpu.VMEM)
    band, size = band_tables()
    flops = 2 * SEGS * count * SAMPLES * SAMPLES * 4
    return pl.pallas_call(
        functools.partial(whiten_kernel, first, count),
        out_shape=jax.ShapeDtypeStruct((SEGS * count, WIDTH), BF16),
        in_specs=[pl.BlockSpec(memory_space=pltpu.SMEM)] + [vmem] * 4,
        out_specs=vmem,
        scratch_shapes=[
            pltpu.SMEM((TEAMS,), jnp.int32),
            pltpu.VMEM((SEGS * count, SAMPLES // 2), F32),
            pltpu.VMEM((SEGS * count, SAMPLES // 2), F32),
            pltpu.VMEM((SEGS * count, LANES), F32),
            pltpu.VMEM((TEAMS, 8, LANES), F32),
            pltpu.VMEM((TEAMS, 8, LANES), F32),
        ],
        compiler_params=pltpu.CompilerParams(vmem_limit_bytes=24 * 2**20),
        cost_estimate=pl.CostEstimate(flops=flops, bytes_accessed=2**23, transcendentals=2**18),
    )(slot_time, received, fourier_tables(), band, size)


def correlate_kernel(sources, first, count, order_ref, *refs):
    own_refs = refs[:len(sources)]
    refs = refs[-6:]
    table_ref, sent_ref, even_ref, odd_ref, cross_ref, scale_ref = refs
    base = first * PLACES
    rows = count * PLACES
    need = rows + HALO
    for (start, length), ref in zip(sources, own_refs):
        low = max(base, start)
        high = min(base + need, start + length)
        for seg in range(SEGS):
            if low < high:
                x = ref[seg * length + low - start:seg * length + high - start].astype(F32)
                even_ref[seg, low - base:high - base] = x
                if low == base:
                    odd_ref[seg, 0:high - low - 4] = x[4:]
                else:
                    odd_ref[seg, low - base - 4:high - base - 4] = x
    tiles = rows // 8

    def round_body(r):
        place = order_ref[r] + 1
        shifted = place % 2
        start = (place - shifted) * PLACES

        def tile_body(ref):
            for t in range(tiles):
                own_rows = pl.ds(8 * t, 8)
                rows_out = pl.ds(pl.multiple_of(r * rows + 8 * t, 8), 8)
                partner_rows = pl.ds(pl.multiple_of(start + 8 * t, 8), 8)
                members = jnp.zeros((8, LANES), F32)
                for seg in range(SEGS):
                    members += even_ref[seg, own_rows, 2 * FREQS:] * ref[seg, partner_rows, 2 * FREQS:]
                scale_ref[rows_out] = 1.0 / jnp.maximum(members, 1.0)
                for c in range(FREQS // LANES):
                    re = slice(c * LANES, (c + 1) * LANES)
                    im = slice(FREQS + c * LANES, FREQS + (c + 1) * LANES)
                    cross_re = jnp.zeros((8, LANES), F32)
                    cross_im = jnp.zeros((8, LANES), F32)
                    for seg in range(SEGS):
                        own_re = even_ref[seg, own_rows, re]
                        own_im = even_ref[seg, own_rows, im]
                        partner_re = ref[seg, partner_rows, re]
                        partner_im = ref[seg, partner_rows, im]
                        cross_re += own_re * partner_re + own_im * partner_im
                        cross_im += own_re * partner_im - own_im * partner_re
                    for where, value in ((re, cross_re), (im, cross_im)):
                        cross_ref[rows_out, where] = value

        @pl.when(shifted == 0)
        def _():
            tile_body(even_ref)

        @pl.when(shifted == 1)
        def _():
            tile_body(odd_ref)

    pl.loop(0, REACH)(round_body)

    def group_body(g):
        both = []
        for i in range(4):
            at = pl.ds(pl.multiple_of((4 * g + i) * rows, 8), rows)
            cross = cross_ref[at]
            large = cross.astype(BF16)
            small = (cross - large.astype(F32)).astype(BF16)
            lagged = dot(large, table_ref[0]) + (dot(large, table_ref[1]) + dot(small, table_ref[0]))
            scale = scale_ref[at]
            lagged = lagged * jnp.concatenate([scale] * (LAGS // LANES), axis=1)
            both.append(lagged.reshape(tiles, 8, LAGS))
        for side in range(2):
            halves = [exchange(both[2 * k], both[2 * k + 1])[side] for k in range(2)]
            block = jnp.concatenate(halves, axis=1).astype(BF16)
            sent_ref[:, side, pl.ds(pl.multiple_of(16 * g, 16), 16)] = block

    for g in range(REACH // 4):
        group_body(g)


def correlate(first, count, round_order, parts, into=None):
    vmem = pl.BlockSpec(memory_space=pltpu.VMEM)
    sources = tuple(where for where, _ in parts)
    arrays = [array for _, array in parts]
    rows = count * PLACES
    base = [] if into is None else [into]
    aliases = {} if into is None else {1 + len(arrays): 0}
    return pl.pallas_call(
        functools.partial(correlate_kernel, sources, first, count),
        grid=(1,),
        out_shape=jax.ShapeDtypeStruct((TEAMS // 2, 2, REACH * PLACES, LAGS), BF16),
        in_specs=[pl.BlockSpec(memory_space=pltpu.SMEM)] + [vmem] * len(arrays)
        + [pl.BlockSpec(memory_space=pl.ANY)] * len(base) + [vmem],
        out_specs=pl.BlockSpec(
            (count // 2, 2, REACH * PLACES, LAGS), lambda i: (first // count, 0, 0, 0)
        ),
        input_output_aliases=aliases,
        scratch_shapes=[
            pltpu.VMEM((SEGS, rows + HALO, WIDTH), F32),
            pltpu.VMEM((SEGS, rows + HALO, WIDTH), F32),
            pltpu.VMEM((REACH * rows, 2 * FREQS), F32),
            pltpu.VMEM((REACH * rows, LANES), F32),
        ],
        compiler_params=pltpu.CompilerParams(vmem_limit_bytes=48 * 2**20),
        cost_estimate=pl.CostEstimate(
            flops=2 * REACH * rows * SAMPLES * LAGS * 6, bytes_accessed=2**22, transcendentals=0
        ),
    )(round_order, *arrays, *base, lag_tables())


def unpack_kernel(flip_ref, owned_ref, out_ref):
    for pair in range(TEAMS // 2):
        at = pair ^ (flip_ref[0] // 2)
        even = owned_ref[at, 0].astype(F32)
        odd = owned_ref[at, 1].astype(F32)
        for half in range(2):
            rows = slice(8 * half, 8 * half + 8)
            for i, tile in enumerate(exchange(even[rows], odd[rows])):
                out_ref[2 * half + i, 8 * pair:8 * pair + 8] = tile


def unpack(flip, owned):
    width = LAGS // 2
    return pl.pallas_call(
        unpack_kernel,
        grid=(REACH // 4, LAGS // width),
        out_shape=jax.ShapeDtypeStruct((REACH, BLOCK, LAGS), F32),
        in_specs=[
            pl.BlockSpec(memory_space=pltpu.SMEM),
            pl.BlockSpec((TEAMS // 2, 2, 16, width), lambda r, l: (0, 0, r, l)),
        ],
        out_specs=pl.BlockSpec((4, BLOCK, width), lambda r, l: (r, 0, l)),
        compiler_params=pltpu.CompilerParams(vmem_limit_bytes=16 * 2**20),
        cost_estimate=pl.CostEstimate(flops=2**20, bytes_accessed=3 * 2**20, transcendentals=0),
    )(flip, owned)


def per_device(recorded, slot_time, passed, round_order):
    groups = lax.axis_size("grp")
    middle = groups // 2
    flip = jnp.where(lax.axis_index("grp") >= middle, MIRROR, 0).astype(jnp.int32).reshape(1)
    route = [
        (g * TEAMS + d, (g - 1) * TEAMS + (d ^ MIRROR if g == middle else d))
        for g in range(1, groups)
        for d in range(TEAMS)
    ]
    pieces = pack(flip, recorded, passed)
    received = lax.all_to_all(pieces, "blk", split_axis=0, concat_axis=0, tiled=True)
    head = whiten(0, HALO, slot_time, received)
    halo = lax.ppermute(head, ("grp", "blk"), route)
    tail = whiten(HALO, ROWS - HALO, slot_time, received)
    parts = [((0, HALO), head), ((HALO, ROWS - HALO), tail), ((ROWS, HALO), halo)]
    inner = TEAMS - REACH
    sent = correlate(0, inner, round_order, parts[:2])
    sent = correlate(inner, REACH, round_order, parts[1:], sent)
    sent = sent.reshape(TEAMS, REACH * PLACES, LAGS)
    owned = lax.all_to_all(sent, "blk", split_axis=0, concat_axis=0, tiled=True)
    return unpack(flip, owned.reshape(TEAMS // 2, 2, REACH * PLACES, LAGS))


def solution(mesh):
    return jax.shard_map(
        per_device,
        mesh=mesh,
        in_specs=(P("grp", "blk"), P(), P(None, ("grp", "blk")), P()),
        out_specs=P(None, ("grp", "blk"), None),
        check_vma=False,
    )
```

```python
import functools
import math

import jax
import jax.numpy as jnp
import numpy as np
from jax import lax
from jax.experimental import pallas as pl
from jax.experimental.pallas import tpu as pltpu
from jax.sharding import PartitionSpec as P

BLOCK = 128
SEGS = 4
SAMPLES = 1024
SLICE = 128
LAGS = 512
HALF = 64
REACH = 8
FREQS = 512
TEAMS = 32
PLACES = BLOCK // TEAMS
ROWS = TEAMS * PLACES
HALO = REACH * PLACES
WIDTH = 2 * FREQS + 128
FLAG = FREQS
LANES = 128
TILES = ROWS // 8
WORD_TILES = 11
WORDS = 8 * WORD_TILES
LOW_BITS = 11
LOW = 2**LOW_BITS - 1
SCALE_BITS = 20
MIDDLE = 2.0**SCALE_BITS
SHRINK = 1.0 - 2.0**-18
SCALE_BASE = 128
MIRROR = 6
EPSILON = 1e-05
F32 = jnp.float32
BF16 = jnp.bfloat16

BINS = np.concatenate([np.arange(0, FREQS, 2), np.arange(1, FREQS, 2)])


def split3(table):
    terms = []
    rest = table.astype(np.float32)
    for _ in range(3):
        term = rest.astype(BF16)
        terms.append(term)
        rest = rest - term.astype(np.float32)
    return terms


def fourier_tables():
    time_index = np.arange(SAMPLES // 2)
    tables = []
    for first in range(2):
        bins = np.arange(first, FREQS, 2)
        angle = (time_index[:, None] * bins[None, :] % SAMPLES) * (2.0 * math.pi / SAMPLES)
        tables.append(split3(np.concatenate([np.cos(angle), -np.sin(angle)], axis=1)))
    return np.stack([np.stack(terms) for terms in tables])


def lag_tables():
    lag_index = np.arange(LAGS) - LAGS // 2
    angle = (BINS[:, None] * lag_index[None, :] % SAMPLES) * (2.0 * math.pi / SAMPLES)
    weight = np.where(BINS == 0, 1.0, 2.0)[:, None] / math.sqrt(SAMPLES)
    table = np.concatenate([weight * np.cos(angle), -weight * np.sin(angle)], axis=0)
    return np.stack(split3(table)[:2])


def band_tables():
    mask = np.abs(BINS[:, None] - BINS[None, :]) <= HALF
    return mask.astype(BF16), (1.0 / mask.sum(axis=0)).astype(np.float32)[None, :]


def low_half(shape):
    return lax.broadcasted_iota(jnp.int32, shape, len(shape) - 2) % 8 < 4


def swap(x):
    return pltpu.roll(x, 4, len(x.shape) - 2)


def exchange(first, second):
    low = low_half(first.shape)
    turned = swap(jnp.where(low, second, first))
    return jnp.where(low, first, turned), jnp.where(low, turned, second)


def dot(a, b):
    return jnp.dot(a, b, preferred_element_type=F32)


def pack_kernel(flip_ref, recorded_ref, passed_ref, pieces_ref, stage_ref, flags_ref, sems):
    parts = sems.shape[0]
    height = BLOCK // parts
    copies = []
    for i in range(parts):
        at = pl.ds(height * i, height)
        copies.append(pltpu.make_async_copy(recorded_ref.at[:, at], stage_ref.at[:, at], sems.at[i]))
        copies[i].start()
    spot = lax.broadcasted_iota(jnp.int32, (BLOCK, LANES), 0)
    lane = lax.broadcasted_iota(jnp.int32, (BLOCK, LANES), 1)
    flags = jnp.zeros((BLOCK, LANES), jnp.int32)
    for seg in range(SEGS):
        line = passed_ref[seg:seg + 1, :].astype(F32)
        column = jnp.sum(jnp.where(spot == lane, line, 0.0), axis=1, keepdims=True)
        flags = jnp.where(lane // TILES == SEGS + seg, column.astype(jnp.int32), flags)
    flags_ref[...] = flags
    lane = lax.broadcasted_iota(jnp.int32, (8, LANES), 1)

    def body(tile):
        at = pl.ds(pl.multiple_of(8 * tile, 8), 8)
        words = []
        for parity in range(2):
            side = flags_ref[at]
            codes = []
            for pair in range(TILES):
                value = stage_ref[2 * pair + parity, at]
                top = jnp.max(jnp.abs(value), axis=1, keepdims=True)
                exponent = jnp.floor(jnp.log2(jnp.maximum(top, 1e-30))) + 1.0
                scale = jnp.exp2(SCALE_BITS - exponent) * SHRINK
                side = jnp.where(lane == pair, exponent.astype(jnp.int32) + SCALE_BASE, side)
                codes.append((value * scale + (MIDDLE + 0.5)).astype(jnp.int32))
            words.append([])
            for k in range(WORD_TILES):
                if k == WORD_TILES - 1:
                    low = side
                elif k % 2 == 0:
                    low = codes[WORD_TILES + k // 2] & LOW
                else:
                    low = lax.shift_right_logical(codes[WORD_TILES + k // 2], LOW_BITS)
                words[parity].append((codes[k] << LOW_BITS) | low)
        for k in range(WORD_TILES):
            for i, word in enumerate(exchange(words[0][k], words[1][k])):
                pieces_ref[(2 * tile + i) ^ flip_ref[0], 8 * k:8 * k + 8] = word

    for i in range(parts):
        copies[i].wait()
        pl.loop(i * height // 8, (i + 1) * height // 8)(body)


def pack(flip, recorded, passed):
    vmem = pl.BlockSpec(memory_space=pltpu.VMEM)
    return pl.pallas_call(
        pack_kernel,
        out_shape=jax.ShapeDtypeStruct((TEAMS, WORDS, SLICE), jnp.int32),
        in_specs=[
            pl.BlockSpec(memory_space=pltpu.SMEM), pl.BlockSpec(memory_space=pltpu.HBM), vmem
        ],
        out_specs=vmem,
        scratch_shapes=[
            pltpu.VMEM((TEAMS, BLOCK, SLICE), F32),
            pltpu.VMEM((BLOCK, LANES), jnp.int32),
            pltpu.SemaphoreType.DMA((4,)),
        ],
        compiler_params=pltpu.CompilerParams(vmem_limit_bytes=16 * 2**20),
        cost_estimate=pl.CostEstimate(flops=2**20, bytes_accessed=2**22, transcendentals=0),
    )(flip, recorded.reshape(TEAMS, BLOCK, SLICE), passed)


def side_tile(received_ref, a):
    return received_ref[a, WORDS - 8:] & LOW


def decode(received_ref, scale_ref, a, t, first):
    if t < WORD_TILES:
        code = lax.shift_right_logical(received_ref[a, 8 * t:8 * t + 8], LOW_BITS)
    else:
        k = 2 * (t - WORD_TILES)
        low = received_ref[a, 8 * k:8 * k + 8] & LOW
        high = received_ref[a, 8 * k + 8:8 * k + 16] & (LOW >> 1)
        code = (high << LOW_BITS) | low
    return (code.astype(F32) - MIDDLE) * scale_ref[pl.ds(pl.multiple_of(8 * a, 8), 8), (t - first) * LANES:(t - first + 1) * LANES]


def flag_tile(side_ref, pair, seg):
    even = side_ref[16 * pair:16 * pair + 8]
    odd = side_ref[16 * pair + 8:16 * pair + 16]
    both = jnp.where(low_half(even.shape), even, odd)
    at = (SEGS + seg) * TILES
    return jnp.broadcast_to(both[:, at:at + 1], (8, LANES))


def whiten_kernel(
    first, count, slot_ref, received_ref, fourier_ref, band_ref, size_ref, white_ref, place_ref, sum_ref, diff_ref,
    flag_ref, side_ref, scale_ref
):
    for a in range(TEAMS):
        place_ref[slot_ref[a]] = a
    for a in range(TEAMS):
        side = side_tile(received_ref, a).astype(F32)
        side_ref[8 * a:8 * a + 8] = side
    own_tiles = count // 8
    source = lax.broadcasted_iota(jnp.int32, (LANES, own_tiles * LANES), 0)
    column = lax.broadcasted_iota(jnp.int32, (LANES, own_tiles * LANES), 1)
    spread = (source == column // LANES + first // 8).astype(BF16)
    exponents = dot(side_ref[...].astype(BF16), spread)
    scale_ref[...] = jnp.exp2(exponents - float(SCALE_BASE + SCALE_BITS)) * (1.0 / SHRINK)
    slices = SAMPLES // SLICE
    half = slices // 2
    for seg in range(SEGS):
        for j in range(half):
            one = place_ref[seg * slices + j]
            other = place_ref[seg * slices + j + half]
            for t in range(count // 8):
                early = decode(received_ref, scale_ref, one, first // 8 + t, first // 8)
                late = decode(received_ref, scale_ref, other, first // 8 + t, first // 8)
                at = seg * count + 8 * t
                sum_ref[at:at + 8, j * SLICE:(j + 1) * SLICE] = early + late
                diff_ref[at:at + 8, j * SLICE:(j + 1) * SLICE] = early - late
        for pair in range(count // 8):
            flag_ref[seg * count + 8 * pair:seg * count + 8 * pair + 8] = flag_tile(
                side_ref, first // 8 + pair, seg
            )
    quarter = FREQS // 2
    rows = SEGS * count

    def transform(x, which):
        x1 = x.astype(BF16)
        rest = x - x1.astype(F32)
        x2 = rest.astype(BF16)
        x3 = (rest - x2.astype(F32)).astype(BF16)
        t1, t2, t3 = (fourier_ref[which, i] for i in range(3))
        first_terms = dot(jnp.concatenate([x1, x2, x3], axis=0), t1)
        second_terms = dot(jnp.concatenate([x1, x2], axis=0), t2)
        small = first_terms[2 * rows:] + second_terms[rows:] + dot(x1, t3)
        return first_terms[:rows] + ((first_terms[rows:2 * rows] + second_terms[:rows]) + small)

    total = sum_ref[...]
    mean = jnp.sum(total, axis=1, keepdims=True) * (1.0 / SAMPLES)
    even = transform(total - 2.0 * mean, 0)
    odd = transform(diff_ref[...], 1)
    parts = (even[:, :quarter], odd[:, :quarter], even[:, quarter:], odd[:, quarter:])
    magnitude = jnp.concatenate(
        [
            jnp.sqrt(parts[0] * parts[0] + parts[2] * parts[2]),
            jnp.sqrt(parts[1] * parts[1] + parts[3] * parts[3]),
        ],
        axis=1,
    )
    large = magnitude.astype(BF16)
    small = (magnitude - large.astype(F32)).astype(BF16)
    level = dot(jnp.concatenate([large, small], axis=0), band_ref[...])
    level = (level[:rows] + level[rows:]) * size_ref[...]
    flags = flag_ref[...]
    scale = jnp.concatenate([flags] * (FREQS // LANES), axis=1) / (level + EPSILON)
    for i, part in enumerate(parts):
        side = scale[:, (i % 2) * quarter:(i % 2 + 1) * quarter]
        white = part * side
        if i * quarter == FLAG:
            lane = lax.broadcasted_iota(jnp.int32, white.shape, 1)
            white = jnp.where(lane == 0, flags[:, :1], white)
        white_ref[:, i * quarter:(i + 1) * quarter] = white.astype(BF16)


def whiten(first, count, slot_time, received):
    vmem = pl.BlockSpec(memory_space=pltpu.VMEM)
    band, size = band_tables()
    flops = 2 * SEGS * count * SAMPLES * SAMPLES * 4
    return pl.pallas_call(
        functools.partial(whiten_kernel, first, count),
        out_shape=jax.ShapeDtypeStruct((SEGS * count, 2 * FREQS), BF16),
        in_specs=[pl.BlockSpec(memory_space=pltpu.SMEM)] + [vmem] * 4,
        out_specs=vmem,
        scratch_shapes=[
            pltpu.SMEM((TEAMS,), jnp.int32),
            pltpu.VMEM((SEGS * count, SAMPLES // 2), F32),
            pltpu.VMEM((SEGS * count, SAMPLES // 2), F32),
            pltpu.VMEM((SEGS * count, LANES), F32),
            pltpu.VMEM((8 * TEAMS, LANES), F32),
            pltpu.VMEM((8 * TEAMS, count // 8 * LANES), F32),
        ],
        compiler_params=pltpu.CompilerParams(vmem_limit_bytes=40 * 2**20),
        cost_estimate=pl.CostEstimate(flops=flops, bytes_accessed=2**23, transcendentals=2**18),
    )(slot_time, received, fourier_tables(), band, size)


def correlate_kernel(sources, first, count, order_ref, *refs):
    own_refs = refs[:len(sources)]
    refs = refs[-5:]
    table_ref, sent_ref, white_ref, cross_ref, scale_ref = refs
    base = first * PLACES
    rows = count * PLACES
    need = rows + HALO
    for (start, length), ref in zip(sources, own_refs):
        low = max(base, start)
        high = min(base + need, start + length)
        for seg in range(SEGS):
            if low < high:
                x = ref[seg * length + low - start:seg * length + high - start].astype(F32)
                edge = x[:, FLAG:FLAG + LANES]
                lane = lax.broadcasted_iota(jnp.int32, edge.shape, 1)
                flags = jnp.broadcast_to(edge[:, :1], edge.shape)
                edge = jnp.where(lane == 0, 0.0, edge)
                x = jnp.concatenate([x[:, :FLAG], edge, x[:, FLAG + LANES:], flags], axis=1)
                white_ref[0, seg, low - base:high - base] = x
                skip = 4 if low == base else 0
                white_ref[1, seg, low - base - 4 + skip:high - base - 4] = x[skip:]
    tiles = rows // 8
    group = 8 if rows < 2 * HALO else 4

    def cross_round(r):
        place = order_ref[r] + 1
        shifted = place % 2
        start = (place - shifted) * PLACES
        for t in range(tiles):
            own_rows = slice(8 * t, 8 * t + 8)
            rows_out = slice(r * rows + 8 * t, r * rows + 8 * t + 8)
            partner_rows = pl.ds(pl.multiple_of(start + 8 * t, 8), 8)
            members = jnp.zeros((8, LANES), F32)
            for seg in range(SEGS):
                own = white_ref[0, seg, own_rows, 2 * FREQS:]
                members += own * white_ref[shifted, seg, partner_rows, 2 * FREQS:]
            scale_ref[rows_out] = 1.0 / jnp.maximum(members, 1.0)
            for c in range(FREQS // LANES):
                re = slice(c * LANES, (c + 1) * LANES)
                im = slice(FREQS + c * LANES, FREQS + (c + 1) * LANES)
                cross_re = jnp.zeros((8, LANES), F32)
                cross_im = jnp.zeros((8, LANES), F32)
                for seg in range(SEGS):
                    own_re = white_ref[0, seg, own_rows, re]
                    own_im = white_ref[0, seg, own_rows, im]
                    partner_re = white_ref[shifted, seg, partner_rows, re]
                    partner_im = white_ref[shifted, seg, partner_rows, im]
                    cross_re += own_re * partner_re + own_im * partner_im
                    cross_im += own_re * partner_im - own_im * partner_re
                cross_ref[rows_out, re] = cross_re
                cross_ref[rows_out, im] = cross_im

    def lag_group(g):
        size = group * rows
        at = slice(g * size, (g + 1) * size)
        cross = cross_ref[at]
        large = cross.astype(BF16)
        small = (cross - large.astype(F32)).astype(BF16)
        both = dot(jnp.concatenate([large, small], axis=0), table_ref[0])
        lagged = both[:size] + (both[size:] + dot(large, table_ref[1]))
        lagged = lagged * jnp.concatenate([scale_ref[at]] * (LAGS // LANES), axis=1)
        rounds = [lagged[i * rows:(i + 1) * rows].reshape(tiles, 8, LAGS) for i in range(group)]
        for side in range(2):
            halves = [exchange(rounds[2 * k], rounds[2 * k + 1])[side] for k in range(group // 2)]
            block = jnp.concatenate(halves, axis=1).astype(BF16)
            sent_ref[:, side, 4 * group * g:4 * group * (g + 1)] = block

    for g in range(REACH // group):
        for i in range(group):
            cross_round(group * g + i)
        lag_group(g)


def correlate(first, count, round_order, parts, into=None):
    vmem = pl.BlockSpec(memory_space=pltpu.VMEM)
    sources = tuple(where for where, _ in parts)
    arrays = [array for _, array in parts]
    rows = count * PLACES
    base = [] if into is None else [into]
    aliases = {} if into is None else {1 + len(arrays): 0}
    return pl.pallas_call(
        functools.partial(correlate_kernel, sources, first, count),
        grid=(1,),
        out_shape=jax.ShapeDtypeStruct((TEAMS // 2, 2, REACH * PLACES, LAGS), BF16),
        in_specs=[pl.BlockSpec(memory_space=pltpu.SMEM)] + [vmem] * len(arrays)
        + [pl.BlockSpec(memory_space=pl.ANY)] * len(base) + [vmem],
        out_specs=pl.BlockSpec(
            (count // 2, 2, REACH * PLACES, LAGS), lambda i: (first // count, 0, 0, 0)
        ),
        input_output_aliases=aliases,
        scratch_shapes=[
            pltpu.VMEM((2, SEGS, rows + HALO, WIDTH), F32),
            pltpu.VMEM((REACH * rows, 2 * FREQS), F32),
            pltpu.VMEM((REACH * rows, LANES), F32),
        ],
        compiler_params=pltpu.CompilerParams(vmem_limit_bytes=48 * 2**20),
        cost_estimate=pl.CostEstimate(
            flops=2 * REACH * rows * SAMPLES * LAGS * 6, bytes_accessed=2**22, transcendentals=0
        ),
    )(round_order, *arrays, *base, lag_tables())


def unpack_kernel(flip_ref, owned_ref, out_ref):
    pairs = out_ref.shape[1] // 8
    part = pl.program_id(1)
    rounds = pl.ds(pl.multiple_of(16 * pl.program_id(0), 16), 16)
    for pair in range(pairs):
        at = (part * pairs + pair) ^ (flip_ref[0] // 2)
        even = owned_ref[at, 0, rounds].astype(F32)
        odd = owned_ref[at, 1, rounds].astype(F32)
        for half in range(2):
            rows = slice(8 * half, 8 * half + 8)
            for i, tile in enumerate(exchange(even[rows], odd[rows])):
                out_ref[2 * half + i, 8 * pair:8 * pair + 8] = tile


def unpack(flip, owned):
    parts = 2
    return pl.pallas_call(
        unpack_kernel,
        grid=(REACH // 4, parts),
        out_shape=jax.ShapeDtypeStruct((REACH, BLOCK, LAGS), F32),
        in_specs=[
            pl.BlockSpec(memory_space=pltpu.SMEM),
            pl.BlockSpec(memory_space=pltpu.VMEM),
        ],
        out_specs=pl.BlockSpec((4, BLOCK // parts, LAGS), lambda r, p: (r, p, 0)),
        compiler_params=pltpu.CompilerParams(vmem_limit_bytes=16 * 2**20),
        cost_estimate=pl.CostEstimate(flops=2**20, bytes_accessed=3 * 2**20, transcendentals=0),
    )(flip, owned)


def per_device(recorded, slot_time, passed, round_order):
    groups = lax.axis_size("grp")
    middle = groups // 2
    flip = jnp.where(lax.axis_index("grp") >= middle, MIRROR, 0).astype(jnp.int32).reshape(1)
    route = [
        (g * TEAMS + d, (g - 1) * TEAMS + (d ^ MIRROR if g == middle else d))
        for g in range(1, groups)
        for d in range(TEAMS)
    ]
    pieces = pack(flip, recorded, passed)
    received = lax.all_to_all(pieces, "blk", split_axis=0, concat_axis=0, tiled=True)
    head = whiten(0, HALO, slot_time, received)
    halo = lax.ppermute(head, ("grp", "blk"), route)
    tail = whiten(HALO, ROWS - HALO, slot_time, received)
    parts = [((0, HALO), head), ((HALO, ROWS - HALO), tail), ((ROWS, HALO), halo)]
    inner = TEAMS - REACH
    sent = correlate(0, inner, round_order, parts[:2])
    sent = correlate(inner, REACH, round_order, parts[1:], sent)
    sent = sent.reshape(TEAMS, REACH * PLACES, LAGS)
    owned = lax.all_to_all(sent, "blk", split_axis=0, concat_axis=0, tiled=True)
    return unpack(flip, owned.reshape(TEAMS // 2, 2, REACH * PLACES, LAGS))


def solution(mesh):
    return jax.shard_map(
        per_device,
        mesh=mesh,
        in_specs=(P("grp", "blk"), P(), P(None, ("grp", "blk")), P()),
        out_specs=P(None, ("grp", "blk"), None),
        check_vma=False,
    )
```

```python
import functools
import math

import jax
import jax.numpy as jnp
import numpy as np
from jax import lax
from jax.experimental import pallas as pl
from jax.experimental.pallas import tpu as pltpu
from jax.sharding import PartitionSpec as P

BLOCK = 128
SEGS = 4
SAMPLES = 1024
SLICE = 128
LAGS = 512
HALF = 64
REACH = 8
FREQS = 512
TEAMS = 32
PLACES = BLOCK // TEAMS
ROWS = TEAMS * PLACES
HALO = REACH * PLACES
WIDTH = 2 * FREQS + 128
FLAG = FREQS
LANES = 128
TILES = ROWS // 8
WORD_TILES = 11
WORDS = 8 * WORD_TILES
LOW_BITS = 11
LOW = 2**LOW_BITS - 1
SCALE_BITS = 20
MIDDLE = 2.0**SCALE_BITS
SHRINK = 1.0 - 2.0**-18
SCALE_BASE = 128
MIRROR = 6
EPSILON = 1e-05
F32 = jnp.float32
BF16 = jnp.bfloat16

BINS = np.concatenate([np.arange(0, FREQS, 2), np.arange(1, FREQS, 2)])


def split3(table):
    terms = []
    rest = table.astype(np.float32)
    for _ in range(3):
        term = rest.astype(BF16)
        terms.append(term)
        rest = rest - term.astype(np.float32)
    return terms


def fourier_tables():
    time_index = np.arange(SAMPLES // 2)
    tables = []
    for first in range(2):
        bins = np.arange(first, FREQS, 2)
        angle = (time_index[:, None] * bins[None, :] % SAMPLES) * (2.0 * math.pi / SAMPLES)
        tables.append(split3(np.concatenate([np.cos(angle), -np.sin(angle)], axis=1)))
    return np.stack([np.stack(terms) for terms in tables])


def lag_tables():
    lag_index = np.arange(LAGS) - LAGS // 2
    angle = (BINS[:, None] * lag_index[None, :] % SAMPLES) * (2.0 * math.pi / SAMPLES)
    weight = np.where(BINS == 0, 1.0, 2.0)[:, None] / math.sqrt(SAMPLES)
    table = np.concatenate([weight * np.cos(angle), -weight * np.sin(angle)], axis=0)
    return np.stack(split3(table)[:2])


def band_tables():
    mask = np.abs(BINS[:, None] - BINS[None, :]) <= HALF
    return mask.astype(BF16), (1.0 / mask.sum(axis=0)).astype(np.float32)[None, :]


def low_half(shape):
    return lax.broadcasted_iota(jnp.int32, shape, len(shape) - 2) % 8 < 4


def swap(x):
    return pltpu.roll(x, 4, len(x.shape) - 2)


def exchange(first, second):
    low = low_half(first.shape)
    turned = swap(jnp.where(low, second, first))
    return jnp.where(low, first, turned), jnp.where(low, turned, second)


def dot(a, b):
    return jnp.dot(a, b, preferred_element_type=F32)


def pack_kernel(flip_ref, recorded_ref, passed_ref, pieces_ref, flags_ref):
    spot = lax.broadcasted_iota(jnp.int32, (BLOCK, LANES), 0)
    lane = lax.broadcasted_iota(jnp.int32, (BLOCK, LANES), 1)
    flags = jnp.zeros((BLOCK, LANES), jnp.int32)
    for seg in range(SEGS):
        line = passed_ref[seg:seg + 1, :].astype(F32)
        column = jnp.sum(jnp.where(spot == lane, line, 0.0), axis=1, keepdims=True)
        flags = jnp.where(lane // TILES == SEGS + seg, column.astype(jnp.int32), flags)
    flags_ref[...] = flags
    lane = lax.broadcasted_iota(jnp.int32, (8, LANES), 1)

    def body(tile):
        at = pl.ds(pl.multiple_of(8 * tile, 8), 8)
        words = []
        for parity in range(2):
            side = flags_ref[at]
            codes = []
            for pair in range(TILES):
                value = recorded_ref[2 * pair + parity, at]
                top = jnp.max(jnp.abs(value), axis=1, keepdims=True)
                exponent = jnp.floor(jnp.log2(jnp.maximum(top, 1e-30))) + 1.0
                scale = jnp.exp2(SCALE_BITS - exponent) * SHRINK
                side = jnp.where(lane == pair, exponent.astype(jnp.int32) + SCALE_BASE, side)
                codes.append((value * scale + (MIDDLE + 0.5)).astype(jnp.int32))
            words.append([])
            for k in range(WORD_TILES):
                if k == WORD_TILES - 1:
                    low = side
                elif k % 2 == 0:
                    low = codes[WORD_TILES + k // 2] & LOW
                else:
                    low = lax.shift_right_logical(codes[WORD_TILES + k // 2], LOW_BITS)
                words[parity].append((codes[k] << LOW_BITS) | low)
        for k in range(WORD_TILES):
            for i, word in enumerate(exchange(words[0][k], words[1][k])):
                pieces_ref[(2 * tile + i) ^ flip_ref[0], 8 * k:8 * k + 8] = word

    pl.loop(0, BLOCK // 8)(body)


def pack(flip, recorded, passed):
    vmem = pl.BlockSpec(memory_space=pltpu.VMEM)
    return pl.pallas_call(
        pack_kernel,
        out_shape=jax.ShapeDtypeStruct((TEAMS, WORDS, SLICE), jnp.int32),
        in_specs=[
            pl.BlockSpec(memory_space=pltpu.SMEM), vmem, vmem
        ],
        out_specs=vmem,
        scratch_shapes=[
            pltpu.VMEM((BLOCK, LANES), jnp.int32),
        ],
        compiler_params=pltpu.CompilerParams(vmem_limit_bytes=16 * 2**20),
        cost_estimate=pl.CostEstimate(flops=2**20, bytes_accessed=2**22, transcendentals=0),
    )(flip, recorded.reshape(TEAMS, BLOCK, SLICE), passed)


def side_tile(received_ref, a):
    return received_ref[a, WORDS - 8:] & LOW


def decode(received_ref, scale_ref, a, t, first):
    if t < WORD_TILES:
        code = lax.shift_right_logical(received_ref[a, 8 * t:8 * t + 8], LOW_BITS)
    else:
        k = 2 * (t - WORD_TILES)
        low = received_ref[a, 8 * k:8 * k + 8] & LOW
        high = received_ref[a, 8 * k + 8:8 * k + 16] & (LOW >> 1)
        code = (high << LOW_BITS) | low
    return (code.astype(F32) - MIDDLE) * scale_ref[pl.ds(pl.multiple_of(8 * a, 8), 8), (t - first) * LANES:(t - first + 1) * LANES]


def flag_tile(side_ref, pair, seg):
    even = side_ref[16 * pair:16 * pair + 8]
    odd = side_ref[16 * pair + 8:16 * pair + 16]
    both = jnp.where(low_half(even.shape), even, odd)
    at = (SEGS + seg) * TILES
    return jnp.broadcast_to(both[:, at:at + 1], (8, LANES))


def whiten_kernel(
    first, count, slot_ref, received_ref, fourier_ref, band_ref, size_ref, white_ref, place_ref, sum_ref, diff_ref,
    flag_ref, side_ref, scale_ref
):
    for a in range(TEAMS):
        place_ref[slot_ref[a]] = a
    for a in range(TEAMS):
        side = side_tile(received_ref, a).astype(F32)
        side_ref[8 * a:8 * a + 8] = side
    own_tiles = count // 8
    source = lax.broadcasted_iota(jnp.int32, (LANES, own_tiles * LANES), 0)
    column = lax.broadcasted_iota(jnp.int32, (LANES, own_tiles * LANES), 1)
    spread = (source == column // LANES + first // 8).astype(BF16)
    exponents = dot(side_ref[...].astype(BF16), spread)
    scale_ref[...] = jnp.exp2(exponents - float(SCALE_BASE + SCALE_BITS)) * (1.0 / SHRINK)
    slices = SAMPLES // SLICE
    half = slices // 2
    for seg in range(SEGS):
        for j in range(half):
            one = place_ref[seg * slices + j]
            other = place_ref[seg * slices + j + half]
            for t in range(count // 8):
                early = decode(received_ref, scale_ref, one, first // 8 + t, first // 8)
                late = decode(received_ref, scale_ref, other, first // 8 + t, first // 8)
                at = seg * count + 8 * t
                sum_ref[at:at + 8, j * SLICE:(j + 1) * SLICE] = early + late
                diff_ref[at:at + 8, j * SLICE:(j + 1) * SLICE] = early - late
        for pair in range(count // 8):
            flag_ref[seg * count + 8 * pair:seg * count + 8 * pair + 8] = flag_tile(
                side_ref, first // 8 + pair, seg
            )
    quarter = FREQS // 2
    rows = SEGS * count

    def transform(x, which):
        x1 = x.astype(BF16)
        rest = x - x1.astype(F32)
        x2 = rest.astype(BF16)
        x3 = (rest - x2.astype(F32)).astype(BF16)
        t1, t2, t3 = (fourier_ref[which, i] for i in range(3))
        first_terms = dot(jnp.concatenate([x1, x2, x3], axis=0), t1)
        second_terms = dot(jnp.concatenate([x1, x2], axis=0), t2)
        small = first_terms[2 * rows:] + second_terms[rows:] + dot(x1, t3)
        return first_terms[:rows] + ((first_terms[rows:2 * rows] + second_terms[:rows]) + small)

    total = sum_ref[...]
    mean = jnp.sum(total, axis=1, keepdims=True) * (1.0 / SAMPLES)
    even = transform(total - 2.0 * mean, 0)
    odd = transform(diff_ref[...], 1)
    parts = (even[:, :quarter], odd[:, :quarter], even[:, quarter:], odd[:, quarter:])
    magnitude = jnp.concatenate(
        [
            jnp.sqrt(parts[0] * parts[0] + parts[2] * parts[2]),
            jnp.sqrt(parts[1] * parts[1] + parts[3] * parts[3]),
        ],
        axis=1,
    )
    large = magnitude.astype(BF16)
    small = (magnitude - large.astype(F32)).astype(BF16)
    level = dot(jnp.concatenate([large, small], axis=0), band_ref[...])
    level = (level[:rows] + level[rows:]) * size_ref[...]
    flags = flag_ref[...]
    scale = jnp.concatenate([flags] * (FREQS // LANES), axis=1) / (level + EPSILON)
    for i, part in enumerate(parts):
        side = scale[:, (i % 2) * quarter:(i % 2 + 1) * quarter]
        white = part * side
        if i * quarter == FLAG:
            lane = lax.broadcasted_iota(jnp.int32, white.shape, 1)
            white = jnp.where(lane == 0, flags[:, :1], white)
        white_ref[:, i * quarter:(i + 1) * quarter] = white.astype(BF16)


def whiten(first, count, slot_time, received):
    vmem = pl.BlockSpec(memory_space=pltpu.VMEM)
    band, size = band_tables()
    flops = 2 * SEGS * count * SAMPLES * SAMPLES * 4
    return pl.pallas_call(
        functools.partial(whiten_kernel, first, count),
        out_shape=jax.ShapeDtypeStruct((SEGS * count, 2 * FREQS), BF16),
        in_specs=[pl.BlockSpec(memory_space=pltpu.SMEM)] + [vmem] * 4,
        out_specs=vmem,
        scratch_shapes=[
            pltpu.SMEM((TEAMS,), jnp.int32),
            pltpu.VMEM((SEGS * count, SAMPLES // 2), F32),
            pltpu.VMEM((SEGS * count, SAMPLES // 2), F32),
            pltpu.VMEM((SEGS * count, LANES), F32),
            pltpu.VMEM((8 * TEAMS, LANES), F32),
            pltpu.VMEM((8 * TEAMS, count // 8 * LANES), F32),
        ],
        compiler_params=pltpu.CompilerParams(vmem_limit_bytes=40 * 2**20),
        cost_estimate=pl.CostEstimate(flops=flops, bytes_accessed=2**23, transcendentals=2**18),
    )(slot_time, received, fourier_tables(), band, size)


def correlate_kernel(sources, first, count, order_ref, *refs):
    own_refs = refs[:len(sources)]
    refs = refs[-5:]
    table_ref, sent_ref, white_ref, cross_ref, scale_ref = refs
    base = first * PLACES
    rows = count * PLACES
    need = rows + HALO
    for (start, length), ref in zip(sources, own_refs):
        low = max(base, start)
        high = min(base + need, start + length)
        for seg in range(SEGS):
            if low < high:
                x = ref[seg * length + low - start:seg * length + high - start].astype(F32)
                edge = x[:, FLAG:FLAG + LANES]
                lane = lax.broadcasted_iota(jnp.int32, edge.shape, 1)
                flags = jnp.broadcast_to(edge[:, :1], edge.shape)
                edge = jnp.where(lane == 0, 0.0, edge)
                x = jnp.concatenate([x[:, :FLAG], edge, x[:, FLAG + LANES:], flags], axis=1)
                white_ref[0, seg, low - base:high - base] = x
                skip = 4 if low == base else 0
                white_ref[1, seg, low - base - 4 + skip:high - base - 4] = x[skip:]
    tiles = rows // 8
    group = 8 if rows < 2 * HALO else 4

    def cross_round(r):
        place = order_ref[r] + 1
        shifted = place % 2
        start = (place - shifted) * PLACES
        for t in range(tiles):
            own_rows = slice(8 * t, 8 * t + 8)
            rows_out = slice(r * rows + 8 * t, r * rows + 8 * t + 8)
            partner_rows = pl.ds(pl.multiple_of(start + 8 * t, 8), 8)
            members = jnp.zeros((8, LANES), F32)
            for seg in range(SEGS):
                own = white_ref[0, seg, own_rows, 2 * FREQS:]
                members += own * white_ref[shifted, seg, partner_rows, 2 * FREQS:]
            scale_ref[rows_out] = 1.0 / jnp.maximum(members, 1.0)
            for c in range(FREQS // LANES):
                re = slice(c * LANES, (c + 1) * LANES)
                im = slice(FREQS + c * LANES, FREQS + (c + 1) * LANES)
                cross_re = jnp.zeros((8, LANES), F32)
                cross_im = jnp.zeros((8, LANES), F32)
                for seg in range(SEGS):
                    own_re = white_ref[0, seg, own_rows, re]
                    own_im = white_ref[0, seg, own_rows, im]
                    partner_re = white_ref[shifted, seg, partner_rows, re]
                    partner_im = white_ref[shifted, seg, partner_rows, im]
                    cross_re += own_re * partner_re + own_im * partner_im
                    cross_im += own_re * partner_im - own_im * partner_re
                cross_ref[rows_out, re] = cross_re
                cross_ref[rows_out, im] = cross_im

    def lag_group(g):
        size = group * rows
        at = slice(g * size, (g + 1) * size)
        cross = cross_ref[at]
        large = cross.astype(BF16)
        small = (cross - large.astype(F32)).astype(BF16)
        both = dot(jnp.concatenate([large, small], axis=0), table_ref[0])
        lagged = both[:size] + (both[size:] + dot(large, table_ref[1]))
        lagged = lagged * jnp.concatenate([scale_ref[at]] * (LAGS // LANES), axis=1)
        rounds = [lagged[i * rows:(i + 1) * rows].reshape(tiles, 8, LAGS) for i in range(group)]
        for side in range(2):
            halves = [exchange(rounds[2 * k], rounds[2 * k + 1])[side] for k in range(group // 2)]
            block = jnp.concatenate(halves, axis=1).astype(BF16)
            sent_ref[:, side, 4 * group * g:4 * group * (g + 1)] = block

    for g in range(REACH // group):
        for i in range(group):
            cross_round(group * g + i)
        lag_group(g)


def correlate(first, count, round_order, parts, into=None):
    vmem = pl.BlockSpec(memory_space=pltpu.VMEM)
    sources = tuple(where for where, _ in parts)
    arrays = [array for _, array in parts]
    rows = count * PLACES
    base = [] if into is None else [into]
    aliases = {} if into is None else {1 + len(arrays): 0}
    return pl.pallas_call(
        functools.partial(correlate_kernel, sources, first, count),
        grid=(1,),
        out_shape=jax.ShapeDtypeStruct((TEAMS // 2, 2, REACH * PLACES, LAGS), BF16),
        in_specs=[pl.BlockSpec(memory_space=pltpu.SMEM)] + [vmem] * len(arrays)
        + [pl.BlockSpec(memory_space=pl.ANY)] * len(base) + [vmem],
        out_specs=pl.BlockSpec(
            (count // 2, 2, REACH * PLACES, LAGS), lambda i: (first // count, 0, 0, 0)
        ),
        input_output_aliases=aliases,
        scratch_shapes=[
            pltpu.VMEM((2, SEGS, rows + HALO, WIDTH), F32),
            pltpu.VMEM((REACH * rows, 2 * FREQS), F32),
            pltpu.VMEM((REACH * rows, LANES), F32),
        ],
        compiler_params=pltpu.CompilerParams(vmem_limit_bytes=48 * 2**20),
        cost_estimate=pl.CostEstimate(
            flops=2 * REACH * rows * SAMPLES * LAGS * 6, bytes_accessed=2**22, transcendentals=0
        ),
    )(round_order, *arrays, *base, lag_tables())


def unpack_kernel(flip_ref, owned_ref, out_ref):
    pairs = out_ref.shape[1] // 8
    part = pl.program_id(1)
    rounds = pl.ds(pl.multiple_of(16 * pl.program_id(0), 16), 16)
    for pair in range(pairs):
        at = (part * pairs + pair) ^ (flip_ref[0] // 2)
        even = owned_ref[at, 0, rounds].astype(F32)
        odd = owned_ref[at, 1, rounds].astype(F32)
        for half in range(2):
            rows = slice(8 * half, 8 * half + 8)
            for i, tile in enumerate(exchange(even[rows], odd[rows])):
                out_ref[2 * half + i, 8 * pair:8 * pair + 8] = tile


def unpack(flip, owned):
    parts = 1
    return pl.pallas_call(
        unpack_kernel,
        grid=(REACH // 4, parts),
        out_shape=jax.ShapeDtypeStruct((REACH, BLOCK, LAGS), F32),
        in_specs=[
            pl.BlockSpec(memory_space=pltpu.SMEM),
            pl.BlockSpec(memory_space=pltpu.VMEM),
        ],
        out_specs=pl.BlockSpec((4, BLOCK // parts, LAGS), lambda r, p: (r, p, 0)),
        compiler_params=pltpu.CompilerParams(vmem_limit_bytes=16 * 2**20),
        cost_estimate=pl.CostEstimate(flops=2**20, bytes_accessed=3 * 2**20, transcendentals=0),
    )(flip, owned)


def per_device(recorded, slot_time, passed, round_order):
    groups = lax.axis_size("grp")
    middle = groups // 2
    flip = jnp.where(lax.axis_index("grp") >= middle, MIRROR, 0).astype(jnp.int32).reshape(1)
    route = [
        (g * TEAMS + d, (g - 1) * TEAMS + (d ^ MIRROR if g == middle else d))
        for g in range(1, groups)
        for d in range(TEAMS)
    ]
    pieces = pack(flip, recorded, passed)
    received = lax.all_to_all(pieces, "blk", split_axis=0, concat_axis=0, tiled=True)
    head = whiten(0, HALO, slot_time, received)
    halo = lax.ppermute(head, ("grp", "blk"), route)
    tail = whiten(HALO, ROWS - HALO, slot_time, received)
    parts = [((0, HALO), head), ((HALO, ROWS - HALO), tail), ((ROWS, HALO), halo)]
    inner = TEAMS - REACH
    sent = correlate(0, inner, round_order, parts[:2])
    sent = correlate(inner, REACH, round_order, parts[1:], sent)
    sent = sent.reshape(TEAMS, REACH * PLACES, LAGS)
    owned = lax.all_to_all(sent, "blk", split_axis=0, concat_axis=0, tiled=True)
    return unpack(flip, owned.reshape(TEAMS // 2, 2, REACH * PLACES, LAGS))


def solution(mesh):
    return jax.shard_map(
        per_device,
        mesh=mesh,
        in_specs=(P("grp", "blk"), P(), P(None, ("grp", "blk")), P()),
        out_specs=P(None, ("grp", "blk"), None),
        check_vma=False,
    )
```

```python
import functools
import math

import jax
import jax.numpy as jnp
import numpy as np
from jax import lax
from jax.experimental import pallas as pl
from jax.experimental.pallas import tpu as pltpu
from jax.sharding import PartitionSpec as P

BLOCK = 128
SEGS = 4
SAMPLES = 1024
SLICE = 128
LAGS = 512
HALF = 64
REACH = 8
FREQS = 512
TEAMS = 32
PLACES = BLOCK // TEAMS
ROWS = TEAMS * PLACES
HALO = REACH * PLACES
WIDTH = 2 * FREQS + 128
FLAG = FREQS
LANES = 128
TILES = ROWS // 8
WORD_TILES = 11
WORDS = 8 * WORD_TILES
LOW_BITS = 11
LOW = 2**LOW_BITS - 1
SCALE_BITS = 20
MIDDLE = 2.0**SCALE_BITS
SHRINK = 1.0 - 2.0**-18
SCALE_BASE = 128
MIRROR = 6
EPSILON = 1e-05
F32 = jnp.float32
BF16 = jnp.bfloat16

BINS = np.concatenate([np.arange(0, FREQS, 2), np.arange(1, FREQS, 2)])


def split3(table):
    terms = []
    rest = table.astype(np.float32)
    for _ in range(3):
        term = rest.astype(BF16)
        terms.append(term)
        rest = rest - term.astype(np.float32)
    return terms


def fourier_tables():
    time_index = np.arange(SAMPLES // 2)
    tables = []
    for first in range(2):
        bins = np.arange(first, FREQS, 2)
        angle = (time_index[:, None] * bins[None, :] % SAMPLES) * (2.0 * math.pi / SAMPLES)
        tables.append(split3(np.concatenate([np.cos(angle), -np.sin(angle)], axis=1)))
    return np.stack([np.stack(terms) for terms in tables])


def lag_tables():
    lag_index = np.arange(LAGS) - LAGS // 2
    angle = (BINS[:, None] * lag_index[None, :] % SAMPLES) * (2.0 * math.pi / SAMPLES)
    weight = np.where(BINS == 0, 1.0, 2.0)[:, None] / math.sqrt(SAMPLES)
    table = np.concatenate([weight * np.cos(angle), -weight * np.sin(angle)], axis=0)
    return np.stack(split3(table)[:2])


def band_tables():
    mask = np.abs(BINS[:, None] - BINS[None, :]) <= HALF
    return mask.astype(BF16), (1.0 / mask.sum(axis=0)).astype(np.float32)[None, :]


def low_half(shape):
    return lax.broadcasted_iota(jnp.int32, shape, len(shape) - 2) % 8 < 4


def swap(x):
    return pltpu.roll(x, 4, len(x.shape) - 2)


def exchange(first, second):
    low = low_half(first.shape)
    turned = swap(jnp.where(low, second, first))
    return jnp.where(low, first, turned), jnp.where(low, turned, second)


def dot(a, b):
    return jnp.dot(a, b, preferred_element_type=F32)


def pack_kernel(flip_ref, recorded_ref, passed_ref, pieces_ref, stage_ref, flags_ref, sems):
    parts = sems.shape[0]
    height = BLOCK // parts
    copies = []
    for i in range(parts):
        at = pl.ds(height * i, height)
        copies.append(pltpu.make_async_copy(recorded_ref.at[:, at], stage_ref.at[:, at], sems.at[i]))
        copies[i].start()
    spot = lax.broadcasted_iota(jnp.int32, (BLOCK, LANES), 0)
    lane = lax.broadcasted_iota(jnp.int32, (BLOCK, LANES), 1)
    flags = jnp.zeros((BLOCK, LANES), jnp.int32)
    for seg in range(SEGS):
        line = passed_ref[seg:seg + 1, :].astype(F32)
        column = jnp.sum(jnp.where(spot == lane, line, 0.0), axis=1, keepdims=True)
        flags = jnp.where(lane // TILES == SEGS + seg, column.astype(jnp.int32), flags)
    flags_ref[...] = flags
    lane = lax.broadcasted_iota(jnp.int32, (8, LANES), 1)

    def body(tile):
        at = pl.ds(pl.multiple_of(8 * tile, 8), 8)
        words = []
        for parity in range(2):
            side = flags_ref[at]
            codes = []
            for pair in range(TILES):
                value = stage_ref[2 * pair + parity, at]
                top = jnp.max(jnp.abs(value), axis=1, keepdims=True)
                exponent = jnp.floor(jnp.log2(jnp.maximum(top, 1e-30))) + 1.0
                scale = jnp.exp2(SCALE_BITS - exponent) * SHRINK
                side = jnp.where(lane == pair, exponent.astype(jnp.int32) + SCALE_BASE, side)
                codes.append((value * scale + (MIDDLE + 0.5)).astype(jnp.int32))
            words.append([])
            for k in range(WORD_TILES):
                if k == WORD_TILES - 1:
                    low = side
                elif k % 2 == 0:
                    low = codes[WORD_TILES + k // 2] & LOW
                else:
                    low = lax.shift_right_logical(codes[WORD_TILES + k // 2], LOW_BITS)
                words[parity].append((codes[k] << LOW_BITS) | low)
        for k in range(WORD_TILES):
            for i, word in enumerate(exchange(words[0][k], words[1][k])):
                pieces_ref[(2 * tile + i) ^ flip_ref[0], 8 * k:8 * k + 8] = word

    for i in range(parts):
        copies[i].wait()
        pl.loop(i * height // 8, (i + 1) * height // 8)(body)


def pack(flip, recorded, passed):
    vmem = pl.BlockSpec(memory_space=pltpu.VMEM)
    return pl.pallas_call(
        pack_kernel,
        out_shape=jax.ShapeDtypeStruct((TEAMS, WORDS, SLICE), jnp.int32),
        in_specs=[
            pl.BlockSpec(memory_space=pltpu.SMEM), pl.BlockSpec(memory_space=pltpu.HBM), vmem
        ],
        out_specs=vmem,
        scratch_shapes=[
            pltpu.VMEM((TEAMS, BLOCK, SLICE), F32),
            pltpu.VMEM((BLOCK, LANES), jnp.int32),
            pltpu.SemaphoreType.DMA((8,)),
        ],
        compiler_params=pltpu.CompilerParams(vmem_limit_bytes=51 * 2**20),
        cost_estimate=pl.CostEstimate(flops=2**20, bytes_accessed=2**22, transcendentals=0),
    )(flip, recorded.reshape(TEAMS, BLOCK, SLICE), passed)


def side_tile(received_ref, a):
    return received_ref[a, WORDS - 8:] & LOW


def decode(received_ref, scale_ref, a, t, first):
    if t < WORD_TILES:
        code = lax.shift_right_logical(received_ref[a, 8 * t:8 * t + 8], LOW_BITS)
    else:
        k = 2 * (t - WORD_TILES)
        low = received_ref[a, 8 * k:8 * k + 8] & LOW
        high = received_ref[a, 8 * k + 8:8 * k + 16] & (LOW >> 1)
        code = (high << LOW_BITS) | low
    return (code.astype(F32) - MIDDLE) * scale_ref[pl.ds(pl.multiple_of(8 * a, 8), 8), (t - first) * LANES:(t - first + 1) * LANES]


def flag_tile(side_ref, pair, seg):
    even = side_ref[16 * pair:16 * pair + 8]
    odd = side_ref[16 * pair + 8:16 * pair + 16]
    both = jnp.where(low_half(even.shape), even, odd)
    at = (SEGS + seg) * TILES
    return jnp.broadcast_to(both[:, at:at + 1], (8, LANES))


def whiten_kernel(
    first, count, slot_ref, received_ref, fourier_ref, band_ref, size_ref, white_ref, place_ref, sum_ref, diff_ref,
    flag_ref, side_ref, scale_ref
):
    for a in range(TEAMS):
        place_ref[slot_ref[a]] = a
    for a in range(TEAMS):
        side = side_tile(received_ref, a).astype(F32)
        side_ref[8 * a:8 * a + 8] = side
    own_tiles = count // 8
    source = lax.broadcasted_iota(jnp.int32, (LANES, own_tiles * LANES), 0)
    column = lax.broadcasted_iota(jnp.int32, (LANES, own_tiles * LANES), 1)
    spread = (source == column // LANES + first // 8).astype(BF16)
    exponents = dot(side_ref[...].astype(BF16), spread)
    scale_ref[...] = jnp.exp2(exponents - float(SCALE_BASE + SCALE_BITS)) * (1.0 / SHRINK)
    slices = SAMPLES // SLICE
    half = slices // 2
    for seg in range(SEGS):
        for j in range(half):
            one = place_ref[seg * slices + j]
            other = place_ref[seg * slices + j + half]
            for t in range(count // 8):
                early = decode(received_ref, scale_ref, one, first // 8 + t, first // 8)
                late = decode(received_ref, scale_ref, other, first // 8 + t, first // 8)
                at = seg * count + 8 * t
                sum_ref[at:at + 8, j * SLICE:(j + 1) * SLICE] = early + late
                diff_ref[at:at + 8, j * SLICE:(j + 1) * SLICE] = early - late
        for pair in range(count // 8):
            flag_ref[seg * count + 8 * pair:seg * count + 8 * pair + 8] = flag_tile(
                side_ref, first // 8 + pair, seg
            )
    quarter = FREQS // 2
    rows = SEGS * count

    def transform(x, which):
        x1 = x.astype(BF16)
        rest = x - x1.astype(F32)
        x2 = rest.astype(BF16)
        x3 = (rest - x2.astype(F32)).astype(BF16)
        t1, t2, t3 = (fourier_ref[which, i] for i in range(3))
        first_terms = dot(jnp.concatenate([x1, x2, x3], axis=0), t1)
        second_terms = dot(jnp.concatenate([x1, x2], axis=0), t2)
        small = first_terms[2 * rows:] + second_terms[rows:] + dot(x1, t3)
        return first_terms[:rows] + ((first_terms[rows:2 * rows] + second_terms[:rows]) + small)

    total = sum_ref[...]
    mean = jnp.sum(total, axis=1, keepdims=True) * (1.0 / SAMPLES)
    even = transform(total - 2.0 * mean, 0)
    odd = transform(diff_ref[...], 1)
    parts = (even[:, :quarter], odd[:, :quarter], even[:, quarter:], odd[:, quarter:])
    magnitude = jnp.concatenate(
        [
            jnp.sqrt(parts[0] * parts[0] + parts[2] * parts[2]),
            jnp.sqrt(parts[1] * parts[1] + parts[3] * parts[3]),
        ],
        axis=1,
    )
    large = magnitude.astype(BF16)
    small = (magnitude - large.astype(F32)).astype(BF16)
    level = dot(jnp.concatenate([large, small], axis=0), band_ref[...])
    level = (level[:rows] + level[rows:]) * size_ref[...]
    flags = flag_ref[...]
    scale = jnp.concatenate([flags] * (FREQS // LANES), axis=1) / (level + EPSILON)
    for i, part in enumerate(parts):
        side = scale[:, (i % 2) * quarter:(i % 2 + 1) * quarter]
        white = part * side
        if i * quarter == FLAG:
            lane = lax.broadcasted_iota(jnp.int32, white.shape, 1)
            white = jnp.where(lane == 0, flags[:, :1], white)
        white_ref[:, i * quarter:(i + 1) * quarter] = white.astype(BF16)


def whiten(first, count, slot_time, received):
    vmem = pl.BlockSpec(memory_space=pltpu.VMEM)
    band, size = band_tables()
    flops = 2 * SEGS * count * SAMPLES * SAMPLES * 4
    return pl.pallas_call(
        functools.partial(whiten_kernel, first, count),
        out_shape=jax.ShapeDtypeStruct((SEGS * count, 2 * FREQS), BF16),
        in_specs=[pl.BlockSpec(memory_space=pltpu.SMEM)] + [vmem] * 4,
        out_specs=vmem,
        scratch_shapes=[
            pltpu.SMEM((TEAMS,), jnp.int32),
            pltpu.VMEM((SEGS * count, SAMPLES // 2), F32),
            pltpu.VMEM((SEGS * count, SAMPLES // 2), F32),
            pltpu.VMEM((SEGS * count, LANES), F32),
            pltpu.VMEM((8 * TEAMS, LANES), F32),
            pltpu.VMEM((8 * TEAMS, count // 8 * LANES), F32),
        ],
        compiler_params=pltpu.CompilerParams(vmem_limit_bytes=40 * 2**20),
        cost_estimate=pl.CostEstimate(flops=flops, bytes_accessed=2**23, transcendentals=2**18),
    )(slot_time, received, fourier_tables(), band, size)


def correlate_kernel(sources, first, count, order_ref, *refs):
    own_refs = refs[:len(sources)]
    refs = refs[-5:]
    table_ref, sent_ref, white_ref, cross_ref, scale_ref = refs
    base = first * PLACES
    rows = count * PLACES
    need = rows + HALO
    for (start, length), ref in zip(sources, own_refs):
        low = max(base, start)
        high = min(base + need, start + length)
        for seg in range(SEGS):
            if low < high:
                x = ref[seg * length + low - start:seg * length + high - start].astype(F32)
                edge = x[:, FLAG:FLAG + LANES]
                lane = lax.broadcasted_iota(jnp.int32, edge.shape, 1)
                flags = jnp.broadcast_to(edge[:, :1], edge.shape)
                edge = jnp.where(lane == 0, 0.0, edge)
                x = jnp.concatenate([x[:, :FLAG], edge, x[:, FLAG + LANES:], flags], axis=1)
                white_ref[0, seg, low - base:high - base] = x
                skip = 4 if low == base else 0
                white_ref[1, seg, low - base - 4 + skip:high - base - 4] = x[skip:]
    tiles = rows // 8
    group = 8 if rows < 2 * HALO else 4

    def cross_round(r):
        place = order_ref[r] + 1
        shifted = place % 2
        start = (place - shifted) * PLACES
        for t in range(tiles):
            own_rows = slice(8 * t, 8 * t + 8)
            rows_out = slice(r * rows + 8 * t, r * rows + 8 * t + 8)
            partner_rows = pl.ds(pl.multiple_of(start + 8 * t, 8), 8)
            members = jnp.zeros((8, LANES), F32)
            for seg in range(SEGS):
                own = white_ref[0, seg, own_rows, 2 * FREQS:]
                members += own * white_ref[shifted, seg, partner_rows, 2 * FREQS:]
            scale_ref[rows_out] = 1.0 / jnp.maximum(members, 1.0)
            for c in range(FREQS // LANES):
                re = slice(c * LANES, (c + 1) * LANES)
                im = slice(FREQS + c * LANES, FREQS + (c + 1) * LANES)
                cross_re = jnp.zeros((8, LANES), F32)
                cross_im = jnp.zeros((8, LANES), F32)
                for seg in range(SEGS):
                    own_re = white_ref[0, seg, own_rows, re]
                    own_im = white_ref[0, seg, own_rows, im]
                    partner_re = white_ref[shifted, seg, partner_rows, re]
                    partner_im = white_ref[shifted, seg, partner_rows, im]
                    cross_re += own_re * partner_re + own_im * partner_im
                    cross_im += own_re * partner_im - own_im * partner_re
                cross_ref[rows_out, re] = cross_re
                cross_ref[rows_out, im] = cross_im

    def lag_group(g):
        size = group * rows
        at = slice(g * size, (g + 1) * size)
        cross = cross_ref[at]
        large = cross.astype(BF16)
        small = (cross - large.astype(F32)).astype(BF16)
        both = dot(jnp.concatenate([large, small], axis=0), table_ref[0])
        lagged = both[:size] + (both[size:] + dot(large, table_ref[1]))
        lagged = lagged * jnp.concatenate([scale_ref[at]] * (LAGS // LANES), axis=1)
        rounds = [lagged[i * rows:(i + 1) * rows].reshape(tiles, 8, LAGS) for i in range(group)]
        for side in range(2):
            halves = [exchange(rounds[2 * k], rounds[2 * k + 1])[side] for k in range(group // 2)]
            block = jnp.concatenate(halves, axis=1).astype(BF16)
            sent_ref[:, side, 4 * group * g:4 * group * (g + 1)] = block

    for g in range(REACH // group):
        for i in range(group):
            cross_round(group * g + i)
        lag_group(g)


def correlate(first, count, round_order, parts, into=None):
    vmem = pl.BlockSpec(memory_space=pltpu.VMEM)
    sources = tuple(where for where, _ in parts)
    arrays = [array for _, array in parts]
    rows = count * PLACES
    base = [] if into is None else [into]
    aliases = {} if into is None else {1 + len(arrays): 0}
    return pl.pallas_call(
        functools.partial(correlate_kernel, sources, first, count),
        grid=(1,),
        out_shape=jax.ShapeDtypeStruct((TEAMS // 2, 2, REACH * PLACES, LAGS), BF16),
        in_specs=[pl.BlockSpec(memory_space=pltpu.SMEM)] + [vmem] * len(arrays)
        + [pl.BlockSpec(memory_space=pl.ANY)] * len(base) + [vmem],
        out_specs=pl.BlockSpec(
            (count // 2, 2, REACH * PLACES, LAGS), lambda i: (first // count, 0, 0, 0)
        ),
        input_output_aliases=aliases,
        scratch_shapes=[
            pltpu.VMEM((2, SEGS, rows + HALO, WIDTH), F32),
            pltpu.VMEM((REACH * rows, 2 * FREQS), F32),
            pltpu.VMEM((REACH * rows, LANES), F32),
        ],
        compiler_params=pltpu.CompilerParams(vmem_limit_bytes=48 * 2**20),
        cost_estimate=pl.CostEstimate(
            flops=2 * REACH * rows * SAMPLES * LAGS * 6, bytes_accessed=2**22, transcendentals=0
        ),
    )(round_order, *arrays, *base, lag_tables())


def unpack_kernel(flip_ref, owned_ref, out_ref):
    pairs = out_ref.shape[1] // 8
    part = pl.program_id(1)
    rounds = pl.ds(pl.multiple_of(16 * pl.program_id(0), 16), 16)
    for pair in range(pairs):
        at = (part * pairs + pair) ^ (flip_ref[0] // 2)
        even = owned_ref[at, 0, rounds].astype(F32)
        odd = owned_ref[at, 1, rounds].astype(F32)
        for half in range(2):
            rows = slice(8 * half, 8 * half + 8)
            for i, tile in enumerate(exchange(even[rows], odd[rows])):
                out_ref[2 * half + i, 8 * pair:8 * pair + 8] = tile


def unpack(flip, owned):
    parts = 1
    return pl.pallas_call(
        unpack_kernel,
        grid=(REACH // 4, parts),
        out_shape=jax.ShapeDtypeStruct((REACH, BLOCK, LAGS), F32),
        in_specs=[
            pl.BlockSpec(memory_space=pltpu.SMEM),
            pl.BlockSpec(memory_space=pltpu.VMEM),
        ],
        out_specs=pl.BlockSpec((4, BLOCK // parts, LAGS), lambda r, p: (r, p, 0)),
        compiler_params=pltpu.CompilerParams(vmem_limit_bytes=16 * 2**20),
        cost_estimate=pl.CostEstimate(flops=2**20, bytes_accessed=3 * 2**20, transcendentals=0),
    )(flip, owned)


def per_device(recorded, slot_time, passed, round_order):
    groups = lax.axis_size("grp")
    middle = groups // 2
    flip = jnp.where(lax.axis_index("grp") >= middle, MIRROR, 0).astype(jnp.int32).reshape(1)
    route = [
        (g * TEAMS + d, (g - 1) * TEAMS + (d ^ MIRROR if g == middle else d))
        for g in range(1, groups)
        for d in range(TEAMS)
    ]
    pieces = pack(flip, recorded, passed)
    received = lax.all_to_all(pieces, "blk", split_axis=0, concat_axis=0, tiled=True)
    head = whiten(0, HALO, slot_time, received)
    halo = lax.ppermute(head, ("grp", "blk"), route)
    tail = whiten(HALO, ROWS - HALO, slot_time, received)
    parts = [((0, HALO), head), ((HALO, ROWS - HALO), tail), ((ROWS, HALO), halo)]
    inner = TEAMS - REACH
    sent = correlate(0, inner, round_order, parts[:2])
    sent = correlate(inner, REACH, round_order, parts[1:], sent)
    sent = sent.reshape(TEAMS, REACH * PLACES, LAGS)
    owned = lax.all_to_all(sent, "blk", split_axis=0, concat_axis=0, tiled=True)
    return unpack(flip, owned.reshape(TEAMS // 2, 2, REACH * PLACES, LAGS))


def solution(mesh):
    return jax.shard_map(
        per_device,
        mesh=mesh,
        in_specs=(P("grp", "blk"), P(), P(None, ("grp", "blk")), P()),
        out_specs=P(None, ("grp", "blk"), None),
        check_vma=False,
    )
```

```python
import functools
import math

import jax
import jax.numpy as jnp
import numpy as np
from jax import lax
from jax.experimental import pallas as pl
from jax.experimental.pallas import tpu as pltpu
from jax.sharding import PartitionSpec as P

BLOCK = 128
SEGS = 4
SAMPLES = 1024
SLICE = 128
LAGS = 512
HALF = 64
REACH = 8
FREQS = 512
TEAMS = 32
PLACES = BLOCK // TEAMS
ROWS = TEAMS * PLACES
HALO = REACH * PLACES
WIDTH = 2 * FREQS + 128
FLAG = FREQS
LANES = 128
TILES = ROWS // 8
WORD_TILES = 11
WORDS = 8 * WORD_TILES
LOW_BITS = 11
LOW = 2**LOW_BITS - 1
SCALE_BITS = 20
MIDDLE = 2.0**SCALE_BITS
SHRINK = 1.0 - 2.0**-18
SCALE_BASE = 128
MIRROR = 6
EPSILON = 1e-05
F32 = jnp.float32
BF16 = jnp.bfloat16

BINS = np.concatenate([np.arange(0, FREQS, 2), np.arange(1, FREQS, 2)])


def split3(table):
    terms = []
    rest = table.astype(np.float32)
    for _ in range(3):
        term = rest.astype(BF16)
        terms.append(term)
        rest = rest - term.astype(np.float32)
    return terms


def fourier_tables():
    time_index = np.arange(SAMPLES // 2)
    tables = []
    for first in range(2):
        bins = np.arange(first, FREQS, 2)
        angle = (time_index[:, None] * bins[None, :] % SAMPLES) * (2.0 * math.pi / SAMPLES)
        tables.append(split3(np.concatenate([np.cos(angle), -np.sin(angle)], axis=1)))
    return np.stack([np.stack(terms) for terms in tables])


def lag_tables():
    lag_index = np.arange(LAGS) - LAGS // 2
    angle = (BINS[:, None] * lag_index[None, :] % SAMPLES) * (2.0 * math.pi / SAMPLES)
    weight = np.where(BINS == 0, 1.0, 2.0)[:, None] / math.sqrt(SAMPLES)
    table = np.concatenate([weight * np.cos(angle), -weight * np.sin(angle)], axis=0)
    return np.stack(split3(table)[:2])


def band_tables():
    mask = np.abs(BINS[:, None] - BINS[None, :]) <= HALF
    return mask.astype(BF16), (1.0 / mask.sum(axis=0)).astype(np.float32)[None, :]


def low_half(shape):
    return lax.broadcasted_iota(jnp.int32, shape, len(shape) - 2) % 8 < 4


def swap(x):
    return pltpu.roll(x, 4, len(x.shape) - 2)


def exchange(first, second):
    low = low_half(first.shape)
    turned = swap(jnp.where(low, second, first))
    return jnp.where(low, first, turned), jnp.where(low, turned, second)


def dot(a, b):
    return jnp.dot(a, b, preferred_element_type=F32)


def pack_kernel(flip_ref, recorded_ref, passed_ref, pieces_ref, stage_ref, flags_ref, sems):
    parts = sems.shape[0]
    height = BLOCK // parts
    copies = []
    for i in range(parts):
        at = pl.ds(height * i, height)
        copies.append(pltpu.make_async_copy(recorded_ref.at[:, at], stage_ref.at[:, at], sems.at[i]))
        copies[i].start()
    spot = lax.broadcasted_iota(jnp.int32, (BLOCK, LANES), 0)
    lane = lax.broadcasted_iota(jnp.int32, (BLOCK, LANES), 1)
    flags = jnp.zeros((BLOCK, LANES), jnp.int32)
    for seg in range(SEGS):
        line = passed_ref[seg:seg + 1, :].astype(F32)
        column = jnp.sum(jnp.where(spot == lane, line, 0.0), axis=1, keepdims=True)
        flags = jnp.where(lane // TILES == SEGS + seg, column.astype(jnp.int32), flags)
    flags_ref[...] = flags
    lane = lax.broadcasted_iota(jnp.int32, (8, LANES), 1)

    def body(tile):
        at = pl.ds(pl.multiple_of(8 * tile, 8), 8)
        words = []
        for parity in range(2):
            side = flags_ref[at]
            codes = []
            for pair in range(TILES):
                value = stage_ref[2 * pair + parity, at]
                top = jnp.max(jnp.abs(value), axis=1, keepdims=True)
                exponent = jnp.floor(jnp.log2(jnp.maximum(top, 1e-30))) + 1.0
                scale = jnp.exp2(SCALE_BITS - exponent) * SHRINK
                side = jnp.where(lane == pair, exponent.astype(jnp.int32) + SCALE_BASE, side)
                codes.append((value * scale + (MIDDLE + 0.5)).astype(jnp.int32))
            words.append([])
            for k in range(WORD_TILES):
                if k == WORD_TILES - 1:
                    low = side
                elif k % 2 == 0:
                    low = codes[WORD_TILES + k // 2] & LOW
                else:
                    low = lax.shift_right_logical(codes[WORD_TILES + k // 2], LOW_BITS)
                words[parity].append((codes[k] << LOW_BITS) | low)
        for k in range(WORD_TILES):
            for i, word in enumerate(exchange(words[0][k], words[1][k])):
                pieces_ref[(2 * tile + i) ^ flip_ref[0], 8 * k:8 * k + 8] = word

    for i in range(parts):
        copies[i].wait()
        pl.loop(i * height // 8, (i + 1) * height // 8)(body)


def pack(flip, recorded, passed):
    vmem = pl.BlockSpec(memory_space=pltpu.VMEM)
    return pl.pallas_call(
        pack_kernel,
        out_shape=jax.ShapeDtypeStruct((TEAMS, WORDS, SLICE), jnp.int32),
        in_specs=[
            pl.BlockSpec(memory_space=pltpu.SMEM), pl.BlockSpec(memory_space=pltpu.HBM), vmem
        ],
        out_specs=vmem,
        scratch_shapes=[
            pltpu.VMEM((TEAMS, BLOCK, SLICE), F32),
            pltpu.VMEM((BLOCK, LANES), jnp.int32),
            pltpu.SemaphoreType.DMA((8,)),
        ],
        compiler_params=pltpu.CompilerParams(vmem_limit_bytes=51 * 2**20),
        cost_estimate=pl.CostEstimate(flops=2**20, bytes_accessed=2**22, transcendentals=0),
    )(flip, recorded.reshape(TEAMS, BLOCK, SLICE), passed)


def side_tile(received_ref, a):
    return received_ref[a, WORDS - 8:] & LOW


def decode(received_ref, scale_ref, a, t, first):
    if t < WORD_TILES:
        code = lax.shift_right_logical(received_ref[a, 8 * t:8 * t + 8], LOW_BITS)
    else:
        k = 2 * (t - WORD_TILES)
        low = received_ref[a, 8 * k:8 * k + 8] & LOW
        high = received_ref[a, 8 * k + 8:8 * k + 16] & (LOW >> 1)
        code = (high << LOW_BITS) | low
    return (code.astype(F32) - MIDDLE) * scale_ref[pl.ds(pl.multiple_of(8 * a, 8), 8), (t - first) * LANES:(t - first + 1) * LANES]


def flag_tile(side_ref, pair, seg):
    even = side_ref[16 * pair:16 * pair + 8]
    odd = side_ref[16 * pair + 8:16 * pair + 16]
    both = jnp.where(low_half(even.shape), even, odd)
    at = (SEGS + seg) * TILES
    return jnp.broadcast_to(both[:, at:at + 1], (8, LANES))


def whiten_kernel(
    first, count, slot_ref, received_ref, fourier_ref, band_ref, size_ref, white_ref, place_ref, sum_ref, diff_ref,
    flag_ref, side_ref, scale_ref
):
    for a in range(TEAMS):
        place_ref[slot_ref[a]] = a
    for a in range(TEAMS):
        side = side_tile(received_ref, a).astype(F32)
        side_ref[8 * a:8 * a + 8] = side
    own_tiles = count // 8
    source = lax.broadcasted_iota(jnp.int32, (LANES, own_tiles * LANES), 0)
    column = lax.broadcasted_iota(jnp.int32, (LANES, own_tiles * LANES), 1)
    spread = (source == column // LANES + first // 8).astype(BF16)
    exponents = dot(side_ref[...].astype(BF16), spread)
    scale_ref[...] = jnp.exp2(exponents - float(SCALE_BASE + SCALE_BITS)) * (1.0 / SHRINK)
    slices = SAMPLES // SLICE
    half = slices // 2
    for seg in range(SEGS):
        for j in range(half):
            one = place_ref[seg * slices + j]
            other = place_ref[seg * slices + j + half]
            for t in range(count // 8):
                early = decode(received_ref, scale_ref, one, first // 8 + t, first // 8)
                late = decode(received_ref, scale_ref, other, first // 8 + t, first // 8)
                at = seg * count + 8 * t
                sum_ref[at:at + 8, j * SLICE:(j + 1) * SLICE] = early + late
                diff_ref[at:at + 8, j * SLICE:(j + 1) * SLICE] = early - late
        for pair in range(count // 8):
            flag_ref[seg * count + 8 * pair:seg * count + 8 * pair + 8] = flag_tile(
                side_ref, first // 8 + pair, seg
            )
    quarter = FREQS // 2
    rows = SEGS * count

    def transform(x, which):
        x1 = x.astype(BF16)
        rest = x - x1.astype(F32)
        x2 = rest.astype(BF16)
        x3 = (rest - x2.astype(F32)).astype(BF16)
        t1, t2, t3 = (fourier_ref[which, i] for i in range(3))
        first_terms = dot(jnp.concatenate([x1, x2, x3], axis=0), t1)
        second_terms = dot(jnp.concatenate([x1, x2], axis=0), t2)
        small = first_terms[2 * rows:] + second_terms[rows:] + dot(x1, t3)
        return first_terms[:rows] + ((first_terms[rows:2 * rows] + second_terms[:rows]) + small)

    total = sum_ref[...]
    mean = jnp.sum(total, axis=1, keepdims=True) * (1.0 / SAMPLES)
    even = transform(total - 2.0 * mean, 0)
    odd = transform(diff_ref[...], 1)
    parts = (even[:, :quarter], odd[:, :quarter], even[:, quarter:], odd[:, quarter:])
    magnitude = jnp.concatenate(
        [
            jnp.sqrt(parts[0] * parts[0] + parts[2] * parts[2]),
            jnp.sqrt(parts[1] * parts[1] + parts[3] * parts[3]),
        ],
        axis=1,
    )
    large = magnitude.astype(BF16)
    small = (magnitude - large.astype(F32)).astype(BF16)
    level = dot(jnp.concatenate([large, small], axis=0), band_ref[...])
    level = (level[:rows] + level[rows:]) * size_ref[...]
    flags = flag_ref[...]
    scale = jnp.concatenate([flags] * (FREQS // LANES), axis=1) / (level + EPSILON)
    for i, part in enumerate(parts):
        side = scale[:, (i % 2) * quarter:(i % 2 + 1) * quarter]
        white = part * side
        if i * quarter == FLAG:
            lane = lax.broadcasted_iota(jnp.int32, white.shape, 1)
            white = jnp.where(lane == 0, flags[:, :1], white)
        white_ref[:, i * quarter:(i + 1) * quarter] = white.astype(BF16)


def whiten(first, count, slot_time, received):
    vmem = pl.BlockSpec(memory_space=pltpu.VMEM)
    band, size = band_tables()
    flops = 2 * SEGS * count * SAMPLES * SAMPLES * 4
    return pl.pallas_call(
        functools.partial(whiten_kernel, first, count),
        out_shape=jax.ShapeDtypeStruct((SEGS * count, 2 * FREQS), BF16),
        in_specs=[pl.BlockSpec(memory_space=pltpu.SMEM)] + [vmem] * 4,
        out_specs=vmem,
        scratch_shapes=[
            pltpu.SMEM((TEAMS,), jnp.int32),
            pltpu.VMEM((SEGS * count, SAMPLES // 2), F32),
            pltpu.VMEM((SEGS * count, SAMPLES // 2), F32),
            pltpu.VMEM((SEGS * count, LANES), F32),
            pltpu.VMEM((8 * TEAMS, LANES), F32),
            pltpu.VMEM((8 * TEAMS, count // 8 * LANES), F32),
        ],
        compiler_params=pltpu.CompilerParams(vmem_limit_bytes=40 * 2**20),
        cost_estimate=pl.CostEstimate(flops=flops, bytes_accessed=2**23, transcendentals=2**18),
    )(slot_time, received, fourier_tables(), band, size)


def correlate_kernel(sources, first, count, order_ref, *refs):
    own_refs = refs[:len(sources)]
    refs = refs[-5:]
    table_ref, sent_ref, white_ref, cross_ref, scale_ref = refs
    base = first * PLACES
    rows = count * PLACES
    need = rows + HALO
    for (start, length), ref in zip(sources, own_refs):
        low = max(base, start)
        high = min(base + need, start + length)
        for seg in range(SEGS):
            if low < high:
                x = ref[seg * length + low - start:seg * length + high - start].astype(F32)
                edge = x[:, FLAG:FLAG + LANES]
                lane = lax.broadcasted_iota(jnp.int32, edge.shape, 1)
                flags = jnp.broadcast_to(edge[:, :1], edge.shape)
                edge = jnp.where(lane == 0, 0.0, edge)
                x = jnp.concatenate([x[:, :FLAG], edge, x[:, FLAG + LANES:], flags], axis=1)
                white_ref[0, seg, low - base:high - base] = x
                skip = 4 if low == base else 0
                white_ref[1, seg, low - base - 4 + skip:high - base - 4] = x[skip:]
    tiles = rows // 8
    group = 8 if rows < 2 * HALO else 4

    def cross_group(rounds):
        places = [order_ref[r] + 1 for r in rounds]
        shifts = [place % 2 for place in places]
        starts = [(place - shifted) * PLACES for place, shifted in zip(places, shifts)]
        for t in range(tiles):
            own_rows = slice(8 * t, 8 * t + 8)
            partners = [pl.ds(pl.multiple_of(start + 8 * t, 8), 8) for start in starts]
            outs = [slice(r * rows + 8 * t, r * rows + 8 * t + 8) for r in rounds]
            own = [white_ref[0, seg, own_rows, 2 * FREQS:] for seg in range(SEGS)]
            for shifted, partner, out in zip(shifts, partners, outs):
                members = jnp.zeros((8, LANES), F32)
                for seg in range(SEGS):
                    members += own[seg] * white_ref[shifted, seg, partner, 2 * FREQS:]
                scale_ref[out] = 1.0 / jnp.maximum(members, 1.0)
            for c in range(FREQS // LANES):
                re = slice(c * LANES, (c + 1) * LANES)
                im = slice(FREQS + c * LANES, FREQS + (c + 1) * LANES)
                own_re = [white_ref[0, seg, own_rows, re] for seg in range(SEGS)]
                own_im = [white_ref[0, seg, own_rows, im] for seg in range(SEGS)]
                for shifted, partner, out in zip(shifts, partners, outs):
                    cross_re = jnp.zeros((8, LANES), F32)
                    cross_im = jnp.zeros((8, LANES), F32)
                    for seg in range(SEGS):
                        partner_re = white_ref[shifted, seg, partner, re]
                        partner_im = white_ref[shifted, seg, partner, im]
                        cross_re += own_re[seg] * partner_re + own_im[seg] * partner_im
                        cross_im += own_re[seg] * partner_im - own_im[seg] * partner_re
                    cross_ref[out, re] = cross_re
                    cross_ref[out, im] = cross_im

    def lag_group(g):
        size = group * rows
        at = slice(g * size, (g + 1) * size)
        cross = cross_ref[at]
        large = cross.astype(BF16)
        small = (cross - large.astype(F32)).astype(BF16)
        both = dot(jnp.concatenate([large, small], axis=0), table_ref[0])
        lagged = both[:size] + (both[size:] + dot(large, table_ref[1]))
        lagged = lagged * jnp.concatenate([scale_ref[at]] * (LAGS // LANES), axis=1)
        rounds = [lagged[i * rows:(i + 1) * rows].reshape(tiles, 8, LAGS) for i in range(group)]
        for side in range(2):
            halves = [exchange(rounds[2 * k], rounds[2 * k + 1])[side] for k in range(group // 2)]
            block = jnp.concatenate(halves, axis=1).astype(BF16)
            sent_ref[:, side, 4 * group * g:4 * group * (g + 1)] = block

    for g in range(REACH // group):
        cross_group(range(group * g, group * (g + 1)))
        lag_group(g)


def correlate(first, count, round_order, parts, into=None):
    vmem = pl.BlockSpec(memory_space=pltpu.VMEM)
    sources = tuple(where for where, _ in parts)
    arrays = [array for _, array in parts]
    rows = count * PLACES
    base = [] if into is None else [into]
    aliases = {} if into is None else {1 + len(arrays): 0}
    return pl.pallas_call(
        functools.partial(correlate_kernel, sources, first, count),
        grid=(1,),
        out_shape=jax.ShapeDtypeStruct((TEAMS // 2, 2, REACH * PLACES, LAGS), BF16),
        in_specs=[pl.BlockSpec(memory_space=pltpu.SMEM)] + [vmem] * len(arrays)
        + [pl.BlockSpec(memory_space=pl.ANY)] * len(base) + [vmem],
        out_specs=pl.BlockSpec(
            (count // 2, 2, REACH * PLACES, LAGS), lambda i: (first // count, 0, 0, 0)
        ),
        input_output_aliases=aliases,
        scratch_shapes=[
            pltpu.VMEM((2, SEGS, rows + HALO, WIDTH), F32),
            pltpu.VMEM((REACH * rows, 2 * FREQS), F32),
            pltpu.VMEM((REACH * rows, LANES), F32),
        ],
        compiler_params=pltpu.CompilerParams(vmem_limit_bytes=48 * 2**20),
        cost_estimate=pl.CostEstimate(
            flops=2 * REACH * rows * SAMPLES * LAGS * 6, bytes_accessed=2**22, transcendentals=0
        ),
    )(round_order, *arrays, *base, lag_tables())


def unpack_kernel(flip_ref, owned_ref, out_ref):
    pairs = out_ref.shape[1] // 8
    part = pl.program_id(1)
    rounds = pl.ds(pl.multiple_of(16 * pl.program_id(0), 16), 16)
    for pair in range(pairs):
        at = (part * pairs + pair) ^ (flip_ref[0] // 2)
        even = owned_ref[at, 0, rounds].astype(F32)
        odd = owned_ref[at, 1, rounds].astype(F32)
        for half in range(2):
            rows = slice(8 * half, 8 * half + 8)
            for i, tile in enumerate(exchange(even[rows], odd[rows])):
                out_ref[2 * half + i, 8 * pair:8 * pair + 8] = tile


def unpack(flip, owned):
    parts = 1
    return pl.pallas_call(
        unpack_kernel,
        grid=(REACH // 4, parts),
        out_shape=jax.ShapeDtypeStruct((REACH, BLOCK, LAGS), F32),
        in_specs=[
            pl.BlockSpec(memory_space=pltpu.SMEM),
            pl.BlockSpec(memory_space=pltpu.VMEM),
        ],
        out_specs=pl.BlockSpec((4, BLOCK // parts, LAGS), lambda r, p: (r, p, 0)),
        compiler_params=pltpu.CompilerParams(vmem_limit_bytes=16 * 2**20),
        cost_estimate=pl.CostEstimate(flops=2**20, bytes_accessed=3 * 2**20, transcendentals=0),
    )(flip, owned)


def per_device(recorded, slot_time, passed, round_order):
    groups = lax.axis_size("grp")
    middle = groups // 2
    flip = jnp.where(lax.axis_index("grp") >= middle, MIRROR, 0).astype(jnp.int32).reshape(1)
    route = [
        (g * TEAMS + d, (g - 1) * TEAMS + (d ^ MIRROR if g == middle else d))
        for g in range(1, groups)
        for d in range(TEAMS)
    ]
    pieces = pack(flip, recorded, passed)
    received = lax.all_to_all(pieces, "blk", split_axis=0, concat_axis=0, tiled=True)
    head = whiten(0, HALO, slot_time, received)
    halo = lax.ppermute(head, ("grp", "blk"), route)
    tail = whiten(HALO, ROWS - HALO, slot_time, received)
    parts = [((0, HALO), head), ((HALO, ROWS - HALO), tail), ((ROWS, HALO), halo)]
    inner = TEAMS - REACH
    sent = correlate(0, inner, round_order, parts[:2])
    sent = correlate(inner, REACH, round_order, parts[1:], sent)
    sent = sent.reshape(TEAMS, REACH * PLACES, LAGS)
    owned = lax.all_to_all(sent, "blk", split_axis=0, concat_axis=0, tiled=True)
    return unpack(flip, owned.reshape(TEAMS // 2, 2, REACH * PLACES, LAGS))


def solution(mesh):
    return jax.shard_map(
        per_device,
        mesh=mesh,
        in_specs=(P("grp", "blk"), P(), P(None, ("grp", "blk")), P()),
        out_specs=P(None, ("grp", "blk"), None),
        check_vma=False,
    )
```
